32 devices in a mesh: scen: 2 (over y), row: 4 (over x, core), col: 4 (over z).
Axes of the slice: x: 2, y: 2, z: 4, core: 2. Of those that a mesh axis runs over, the one named last changes fastest.
Arguments:
- tokens: bfloat16 [10240, 4096], P(('scen', 'row'), 'col'), parts along dimension 0, may hold values from -60 to 60
- norm_gain: float32 [4096], replicated, may hold values from 0.1 to 1.9
- w_in: bfloat16 [4096, 16384], P('row', 'col'), may hold values from -0.09375 to 0.09375
- conv_kernel: float32 [9, 16384], P(None, 'col'), may hold values from -2 to 2
- w_out: bfloat16 [16384, 4096], P('col', 'row'), may hold values from -0.0625 to 0.0625
Outputs:
- block_out: bfloat16 [10240, 4096], P(('scen', 'row'), 'col'), parts along dimension 0
The draws below stay inside these ranges and needn't reach their ends.
There are 2 independent parts, one for each index of `scen`. The reference program is written for one: setup_inputs(seed, part) draws one part's arguments, and reference() takes and returns one part's arrays. A program takes and returns all parts, laid end to end along the dimension named above; an argument that names none is the same for every part. Nothing has to cross between parts.
All inputs are finite; a program needn't handle non-finite values.
Results may differ from the reference program's by a relative error of at most 0.0038.
Values may be sent and summed in bfloat16 or wider, within the bound.
No kernel may reach another device: no remote copies, remote signals or barrier semaphores. Data moves between devices by JAX's collectives and lax.ppermute only.
A program may use at most 192 MiB of HBM per device.

```python
import math
import jax
import jax.numpy as jnp
from jax import lax

D = 4096
FF = 16384
LON = 128
LAT = 40
TOKENS = 5120


def draw_tokens(key, part):
    first, second, third = jax.random.split(key, 3)
    row_scale = jnp.exp(jax.random.uniform(first, (TOKENS, 1), jnp.float32, math.log(0.5), math.log(5.0)))
    col_scale = jnp.exp(jax.random.uniform(second, (1, D), jnp.float32, math.log(0.3), math.log(3.0)))
    base = jax.random.normal(third, (TOKENS, D), jnp.float32)
    base = jnp.clip(base, -4.0, 4.0)
    return (base * row_scale * col_scale).astype(jnp.bfloat16)


def with_spikes(drawn, own_key, source, target, parts, factor):
    def block_of(dim):
        return (jnp.arange(drawn.shape[dim]) // (drawn.shape[dim] // parts)).reshape((-1,) + (1,) * (drawn.ndim - 1 - dim))

    one_side = jax.random.permutation(own_key, parts)[block_of(target)]
    far = (block_of(target) + parts // 2) % parts
    return jnp.where((block_of(source) == one_side) | (block_of(source) == far), factor * drawn, drawn)


def block_levels(key, extent, cuts, least, high):
    gain, own = 1.0, jax.random.fold_in(key, 6)
    for axis_at, parts in cuts:
        steps = jnp.exp(jax.random.uniform(jax.random.fold_in(own, axis_at), (parts,), jnp.float32, least / len(cuts), high / len(cuts)))
        gain = gain * jnp.repeat(steps, extent[axis_at] // parts).reshape([-1 if axis == axis_at else 1 for axis in range(len(extent))])
    return gain


def centred(key, extent, scale, reach, cuts=(), dtype=jnp.bfloat16):
    level = block_levels(key, extent, cuts, -0.22, 0.18) if cuts else 1.0
    drawn = jax.random.normal(key, extent, jnp.float32) * scale * level
    return jnp.minimum(jnp.maximum(drawn, -reach), reach).astype(dtype)


def gaussian_with(own_key, dims, deviation, reach, cuts, heavy, dtype=jnp.bfloat16):
    drawn = deviation * jax.random.normal(own_key, dims, jnp.float32)
    if cuts:
        drawn = drawn * block_levels(own_key, dims, cuts, -0.22, 0.18)
    return jnp.clip(with_spikes(drawn, jax.random.fold_in(own_key, 3), *heavy), -reach, reach).astype(dtype)


def setup_inputs(seed: int = 0, part: int = 0) -> dict:
    streams_of = jax.random.split(jax.random.key(seed), 6)
    own_keys = jax.random.split(jax.random.fold_in(streams_of[5], part), 6)
    tokens = draw_tokens(jax.random.fold_in(jax.random.fold_in(streams_of[5], part), 71), part)
    norm_gain = jnp.clip(1.0 + 0.18 * jax.random.normal(streams_of[1], (D,), jnp.float32), 0.1, 1.9)
    w_in = centred(streams_of[2], (D, FF), D ** -0.5, 0.09375, ((0, 4), (1, 4)))
    conv_kernel = centred(streams_of[3], (9, FF), 0.33, 2.0, ((1, 4),), jnp.float32)
    w_out = gaussian_with(streams_of[4], (FF, D), FF ** -0.5, 0.0625, ((0, 4), (1, 4)), (0, 1, 4, 2.0))
    return {"tokens": tokens, "norm_gain": norm_gain, "w_in": w_in, "conv_kernel": conv_kernel, "w_out": w_out}


eps = 1e-05

def reference(tokens, norm_gain, w_in, conv_kernel, w_out):
    values = tokens.astype(jnp.float32)
    mean = lax.optimization_barrier(jnp.mean(values, axis=1, keepdims=True))
    var = lax.optimization_barrier(jnp.mean(values * values, axis=1, keepdims=True)) - mean * mean
    normed = ((values - mean) * lax.rsqrt(var + eps) * norm_gain).astype(jnp.bfloat16)
    hidden = jnp.dot(normed, w_in, preferred_element_type=jnp.float32).astype(jnp.bfloat16)
    grid = hidden.reshape(LON, LAT, FF).astype(jnp.float32)
    grid = jnp.concatenate([grid[-1:], grid, grid[:1]], axis=0)
    grid = jnp.pad(grid, ((0, 0), (1, 1), (0, 0)))
    conv = jnp.zeros((LON, LAT, FF), jnp.float32)
    for shift_lon in range(3):
        for shift_lat in range(3):
            conv = conv + conv_kernel[shift_lon * 3 + shift_lat] * grid[shift_lon:shift_lon + LON, shift_lat:shift_lat + LAT]
    act = jax.nn.gelu(conv, approximate=True).astype(jnp.bfloat16).reshape(LON * LAT, FF)
    mixed = jnp.dot(act, w_out, preferred_element_type=jnp.float32)
    return (values + mixed).astype(jnp.bfloat16)
```

```python
import functools

import jax
import jax.numpy as jnp
from jax import lax
from jax.experimental import pallas as pl
from jax.experimental.pallas import tpu as pltpu
from jax.sharding import PartitionSpec as P

LAT = 40
eps = 1e-05
TILE = 512
VMEM_LIMIT = 44 * 1024 * 1024


def extended(cells, sides, width):
    for axis, dim in sides:
        count = lax.axis_size(axis)
        head = lax.slice_in_dim(cells, 0, width, axis=dim)
        tail = lax.slice_in_dim(cells, cells.shape[dim] - width, cells.shape[dim], axis=dim)
        cells = jnp.concatenate(
            [
                lax.ppermute(tail, axis, [(i, (i + 1) % count) for i in range(count)]),
                cells,
                lax.ppermute(head, axis, [((i + 1) % count, i) for i in range(count)]),
            ],
            axis=dim,
        )
    return cells


def any_mesh(tokens, norm_gain, w_in, conv_kernel, w_out):
    rows, local_cols = tokens.shape
    values = tokens.astype(jnp.float32)
    whole = lax.all_gather(tokens, "col", axis=1, tiled=True).astype(jnp.float32)
    mean = jnp.mean(whole, axis=1, keepdims=True)
    var = jnp.mean(whole * whole, axis=1, keepdims=True) - mean * mean
    normed = ((whole - mean) * lax.rsqrt(var + eps) * norm_gain).astype(jnp.bfloat16)
    units = w_in.shape[1]
    pre_hidden = jnp.dot(
        normed, lax.all_gather(w_in, "row", axis=0, tiled=True), preferred_element_type=jnp.float32
    )
    hidden = pre_hidden.astype(jnp.bfloat16)
    lon_local = rows // LAT
    grid = hidden.reshape(lon_local, LAT, units)
    padded = extended(grid, (("row", 0),), 1)
    padded = jnp.pad(padded.astype(jnp.float32), ((0, 0), (1, 1), (0, 0)))
    conv = jnp.zeros((lon_local, LAT, units), jnp.float32)
    for shift_lon in range(3):
        for shift_lat in range(3):
            conv = (
                conv
                + conv_kernel[shift_lon * 3 + shift_lat]
                * padded[shift_lon : shift_lon + lon_local, shift_lat : shift_lat + LAT]
            )
    act = jax.nn.gelu(conv, approximate=True).astype(jnp.bfloat16).reshape(rows, units)
    partial_value = jnp.dot(
        act, lax.all_gather(w_out, "row", axis=1, tiled=True), preferred_element_type=jnp.float32
    )
    mixed = lax.psum_scatter(partial_value, "col", scatter_dimension=1, tiled=True)
    return (values + mixed).astype(jnp.bfloat16)


def after(value, *others):
    return lax.optimization_barrier((value, *others))[0]


def swap_x(v):
    return lax.ppermute(v, "row", [(i, i ^ 2) for i in range(4)])


def swap_core(v):
    return lax.ppermute(v, "row", [(i, i ^ 1) for i in range(4)])


def swap_scen(v):
    return lax.ppermute(v, "scen", [(0, 1), (1, 0)])


def down(v, hop):
    return lax.ppermute(v, "col", [(i, i - 1) for i in range(1, 5 - hop)])


def up(v, hop):
    return lax.ppermute(v, "col", [(i, i + 1) for i in range(hop - 1, 3)])


def spread(own, first):
    own_ = after(own, *first)
    d, u = [], []
    dv, uv = own_, own_
    for hop in (1, 2, 3):
        dv, uv = down(dv, hop), up(uv, hop)
        d.append(dv)
        u.append(uv)
        dv, uv = lax.optimization_barrier((dv, uv))
    return [own, *d, *u]


def conv_gelu(hid_ref, k_ref, o_ref, lons):
    width = hid_ref.shape[1]
    lanes = 256
    for c in range(0, width, lanes):
        cols = pl.ds(c, lanes)
        taps = [k_ref[pl.ds(i, 1), cols] for i in range(9)]
        at = lax.broadcasted_iota(jnp.int32, (LAT, lanes), 0)

        def one_lon(lon):
            base = pl.multiple_of(lon * LAT, 8)
            left = hid_ref[pl.ds(base, LAT), cols]
            here = hid_ref[pl.ds(pl.multiple_of(base + LAT, 8), LAT), cols]
            right = hid_ref[pl.ds(pl.multiple_of(base + 2 * LAT, 8), LAT), cols]
            s = [taps[b] * left + taps[3 + b] * here + taps[6 + b] * right for b in range(3)]
            below = jnp.where(at == 0, 0.0, pltpu.roll(s[0], 1, 0))
            above = jnp.where(at == LAT - 1, 0.0, pltpu.roll(s[2], LAT - 1, 0))
            v = s[1] + below + above
            inner = 0.7978845608028654 * (v + 0.044715 * (v * v * v))
            return 0.5 * v * (1.0 + jnp.tanh(inner))

        def one(pair, _):
            both = jnp.concatenate([one_lon(2 * pair), one_lon(2 * pair + 1)], axis=0)
            o_ref[pl.ds(pl.multiple_of(pair * 2 * LAT, 16), 2 * LAT), cols] = both.astype(o_ref.dtype)
            return 0

        lax.fori_loop(0, lons // 2, one, 0)


def first_kernel(has_tail, n_w, place_ref, *refs):
    toks, refs = refs[:7], refs[7:]
    ws, refs = refs[:n_w], refs[n_w:]
    if has_tail:
        tail_ref, k_ref, act_ref, tok, wbuf, hid, tsem, wsem = refs
    else:
        k_ref, act_ref, tail_out, tok, wbuf, hid, tsem, wsem = refs
    scen, row, col = place_ref[0], place_ref[1], place_ref[2]
    n, count = pl.program_id(0), pl.num_programs(0)
    d = toks[0].shape[1]

    def w_copies(tile, slot):
        cols = pl.ds(pl.multiple_of(tile * TILE, TILE), TILE)
        for ref, base, step, flip in ws_places(ws):
            off = base + step * (scen if not flip else 1 - scen)
            off = pl.multiple_of(jnp.int32(off), 16)
            pltpu.make_async_copy(
                ref.at[:, cols], wbuf.at[slot, pl.ds(off, ref.shape[0]), :], wsem.at[slot]
            ).start()

    @pl.when(n == 0)
    def _():
        w_copies(0, 0)

        def tok_copy(ref, f):
            at = pl.multiple_of((row ^ f) * d, d)
            pltpu.make_async_copy(ref, tok.at[:, pl.ds(at, d)], tsem).start()

        tok_copy(toks[0], col)
        for hop in (1, 2, 3):

            @pl.when(col + hop <= 3)
            def _():
                tok_copy(toks[hop], col + hop)

            @pl.when(col - hop >= 0)
            def _():
                tok_copy(toks[3 + hop], col - hop)

        pltpu.make_async_copy(tok, tok, tsem).wait()

    slot = lax.rem(n, 2)

    @pl.when(n + 1 < count)
    def _():
        w_copies(n + 1, 1 - slot)

    pltpu.make_async_copy(wbuf.at[slot], wbuf.at[slot], wsem.at[slot]).wait()
    lead = hid.shape[0] - tok.shape[0]
    if has_tail:
        hid[pl.ds(0, lead), :] = tail_ref[...].astype(jnp.float32)
    product = jnp.dot(tok[...], wbuf[slot], preferred_element_type=jnp.float32)
    hidden = product.astype(jnp.bfloat16)
    if not has_tail:
        tail_out[...] = hidden[hidden.shape[0] - 2 * LAT :]
    hid[pl.ds(lead, tok.shape[0]), :] = hidden.astype(jnp.float32)
    conv_gelu(hid, k_ref, act_ref, act_ref.shape[0] // LAT)


def ws_places(ws):
    d = ws[0].shape[0]
    own, sib = ws[:2]
    out = [(own, 0, 0, False), (sib, d, 0, False)]
    pieces = (len(ws) - 2) // 2
    for which in range(2):
        mine = ws[2 + which * pieces : 2 + (which + 1) * pieces]
        base = (2 + which) * d
        x0, y0, x1, y1 = mine[:4]
        h = x0.shape[0]
        out += [(x0, base, 2 * h, False), (y0, base, 2 * h, True)]
        out += [(x1, base + h, 2 * h, False), (y1, base + h, 2 * h, True)]
        if len(mine) > 4:
            out += [(mine[4], base + 4 * h, 0, False)]
    return out


def first(place, toks, ws, conv_kernel, tail, lons):
    rows, d = toks[0].shape
    units = conv_kernel.shape[1]
    has_tail = tail is not None
    hid_rows = rows + (2 * LAT if has_tail else 0)
    out_rows = lons * LAT
    any_spec = pl.BlockSpec(memory_space=pl.ANY)
    wide = lambda r: pl.BlockSpec((r, TILE), lambda n: (0, n))
    act_shape = jax.ShapeDtypeStruct((out_rows, units), jnp.bfloat16)
    tail_shape = jax.ShapeDtypeStruct((2 * LAT, units), jnp.bfloat16)
    return pl.pallas_call(
        functools.partial(first_kernel, has_tail, len(ws)),
        grid=(units // TILE,),
        in_specs=[pl.BlockSpec(memory_space=pltpu.SMEM)]
        + [any_spec] * (7 + len(ws))
        + ([wide(2 * LAT)] if has_tail else [])
        + [wide(9)],
        out_specs=wide(out_rows) if has_tail else [wide(out_rows), wide(2 * LAT)],
        out_shape=act_shape if has_tail else [act_shape, tail_shape],
        scratch_shapes=[
            pltpu.VMEM((rows, 4 * d), jnp.bfloat16),
            pltpu.VMEM((2, 4 * d, TILE), jnp.bfloat16),
            pltpu.VMEM((hid_rows, TILE), jnp.float32),
            pltpu.SemaphoreType.DMA,
            pltpu.SemaphoreType.DMA((2,)),
        ],
        compiler_params=pltpu.CompilerParams(vmem_limit_bytes=VMEM_LIMIT),
        cost_estimate=pl.CostEstimate(
            flops=2 * rows * 4 * d * units, bytes_accessed=8 * d * units, transcendentals=0
        ),
        name="first",
    )(place, *toks, *ws, *([tail] if has_tail else []), conv_kernel)


def w_in_parts(w, scen, start):
    d, units = w.shape
    h = (d * 13 // 64) // 16 * 16
    x_in = [lax.dynamic_slice(w, (scen * 2 * h + i * h, 0), (h, units)) for i in range(2)]
    sib = swap_core(w)
    x0 = swap_x(x_in[0])
    x1 = swap_x(after(x_in[1], x0))
    y0 = swap_scen(x0)
    xd = swap_x(after(w[4 * h :], x1))
    y1 = swap_scen(after(x1, y0))
    mine = [x0, y0, x1, y1, xd]
    return [w, sib, *mine, *[swap_core(v) for v in mine]], (x1, xd, y1)


def per_device(tokens, norm_gain, w_in, conv_kernel, w_out):
    rows, d = tokens.shape
    scen, row, col = (lax.axis_index(a) for a in ("scen", "row", "col"))
    place = jnp.stack([scen, row, col]).astype(jnp.int32)
    wide = extended(tokens, (("row", 0),), LAT)
    v = wide.astype(jnp.float32)
    sums = jnp.stack([jnp.sum(v, axis=1), jnp.sum(v * v, axis=1)])
    sums = jnp.sum(lax.all_gather(sums, "col"), axis=0) / (4 * d)
    mean = sums[0][:, None]
    var = sums[1][:, None] - mean * mean
    gain = lax.dynamic_slice(norm_gain, (col * d,), (d,))
    normed = ((v - mean) * lax.rsqrt(var + eps) * gain).astype(jnp.bfloat16)

    lons = rows // LAT
    cut = (lons // 2 + 2) * LAT
    toks_a = spread(normed[:cut], ())
    toks_b = spread(normed[cut:], toks_a[1:])

    ws, (x1, xd, y1) = w_in_parts(w_in, scen, ())
    act_a, tail = first(place, toks_a, ws, conv_kernel, None, lons // 2)
    act_b = first(place, toks_b, ws, conv_kernel, tail, lons - lons // 2)

    q = d // 4
    out_in = [lax.dynamic_slice(w_out, (0, i * 2 * q + scen * q), (w_out.shape[0], q)) for i in range(2)]
    o_sib = swap_core(after(w_out, ws[1]))
    ox0 = swap_x(after(out_in[0], xd))
    oy0 = swap_scen(after(ox0, y1))
    ox1 = swap_x(after(out_in[1], ox0))
    oy1 = swap_scen(after(ox1, oy0))

    def join(a, b):
        return jnp.concatenate([jnp.where(scen == 0, a, b), jnp.where(scen == 0, b, a)], axis=1)

    far = jnp.concatenate([join(ox0, oy0), join(ox1, oy1)], axis=1)
    far_sib = swap_core(far)
    shards = jnp.stack([w_out, o_sib, far, far_sib])
    full = jnp.concatenate([lax.dynamic_index_in_dim(shards, row ^ f, 0, False) for f in range(4)], axis=1)
    outs = []
    for act in (act_a, act_b):
        part = jnp.dot(act, full, preferred_element_type=jnp.float32).astype(jnp.bfloat16)
        outs.append(lax.psum_scatter(part, "col", scatter_dimension=1, tiled=True))
    mixed = jnp.concatenate(outs, axis=0).astype(jnp.float32)
    return (tokens.astype(jnp.float32) + mixed).astype(jnp.bfloat16)


def solution(mesh):
    placed = (P(("scen", "row"), "col"), P(), P("row", "col"), P(None, "col"), P("col", "row"))
    sizes = tuple(mesh.shape[a] for a in ("scen", "row", "col"))
    return jax.shard_map(
        per_device if sizes == (2, 4, 4) else any_mesh,
        mesh=mesh,
        in_specs=placed,
        out_specs=P(("scen", "row"), "col"),
        check_vma=False,
    )
```

```python
import functools

import jax
import jax.numpy as jnp
from jax import lax
from jax.experimental import pallas as pl
from jax.experimental.pallas import tpu as pltpu
from jax.sharding import PartitionSpec as P

LAT = 40
eps = 1e-05
TILE = 1024
SUB = 512
LANES = 128
BLOCK = 80
VMEM_LIMIT = 58 * 1024 * 1024


def extended(cells, sides, width):
    for axis, dim in sides:
        count = lax.axis_size(axis)
        head = lax.slice_in_dim(cells, 0, width, axis=dim)
        tail = lax.slice_in_dim(cells, cells.shape[dim] - width, cells.shape[dim], axis=dim)
        cells = jnp.concatenate(
            [
                lax.ppermute(tail, axis, [(i, (i + 1) % count) for i in range(count)]),
                cells,
                lax.ppermute(head, axis, [((i + 1) % count, i) for i in range(count)]),
            ],
            axis=dim,
        )
    return cells


def any_mesh(tokens, norm_gain, w_in, conv_kernel, w_out):
    rows, local_cols = tokens.shape
    values = tokens.astype(jnp.float32)
    whole = lax.all_gather(tokens, "col", axis=1, tiled=True).astype(jnp.float32)
    mean = jnp.mean(whole, axis=1, keepdims=True)
    var = jnp.mean(whole * whole, axis=1, keepdims=True) - mean * mean
    normed = ((whole - mean) * lax.rsqrt(var + eps) * norm_gain).astype(jnp.bfloat16)
    units = w_in.shape[1]
    pre_hidden = jnp.dot(
        normed, lax.all_gather(w_in, "row", axis=0, tiled=True), preferred_element_type=jnp.float32
    )
    hidden = pre_hidden.astype(jnp.bfloat16)
    lon_local = rows // LAT
    grid = hidden.reshape(lon_local, LAT, units)
    padded = extended(grid, (("row", 0),), 1)
    padded = jnp.pad(padded.astype(jnp.float32), ((0, 0), (1, 1), (0, 0)))
    conv = jnp.zeros((lon_local, LAT, units), jnp.float32)
    for shift_lon in range(3):
        for shift_lat in range(3):
            conv = (
                conv
                + conv_kernel[shift_lon * 3 + shift_lat]
                * padded[shift_lon : shift_lon + lon_local, shift_lat : shift_lat + LAT]
            )
    act = jax.nn.gelu(conv, approximate=True).astype(jnp.bfloat16).reshape(rows, units)
    partial_value = jnp.dot(
        act, lax.all_gather(w_out, "row", axis=1, tiled=True), preferred_element_type=jnp.float32
    )
    mixed = lax.psum_scatter(partial_value, "col", scatter_dimension=1, tiled=True)
    return (values + mixed).astype(jnp.bfloat16)


def after(value, *others):
    return lax.optimization_barrier((value, *others))[0]


def swap_x(v):
    return lax.ppermute(v, "row", [(i, i ^ 2) for i in range(4)])


def swap_core(v):
    return lax.ppermute(v, "row", [(i, i ^ 1) for i in range(4)])


def cores(*values):
    out = []
    for v in values:
        out.append(swap_core(after(v, *out[-1:])))
    return out


def swap_scen(v):
    return lax.ppermute(v, "scen", [(0, 1), (1, 0)])


def down(v, hop):
    return lax.ppermute(v, "col", [(i, i - 1) for i in range(1, 5 - hop)])


def up(v, hop):
    return lax.ppermute(v, "col", [(i, i + 1) for i in range(hop - 1, 3)])


def gate(done, begin):
    done, begin = lax.optimization_barrier((tuple(done), tuple(begin)))
    return list(done), list(begin)


def conv_gelu(hid_ref, k_ref, o_ref, col, lons):
    for c in range(0, hid_ref.shape[1], LANES):
        conv_gelu_lanes(hid_ref, k_ref, o_ref, c, col + c, lons)


def conv_gelu_lanes(hid_ref, k_ref, o_ref, lane, col, lons):
    width = LANES
    cols, here_cols = pl.ds(col, width), pl.ds(lane, width)
    taps = [k_ref[pl.ds(i, 1), cols] for i in range(9)]
    at = lax.broadcasted_iota(jnp.int32, (LAT, width), 0)

    def one_lon(lon):
        left, here, right = (hid_ref[pl.ds((lon + a) * LAT, LAT), here_cols] for a in range(3))
        s = [taps[b] * left + taps[3 + b] * here + taps[6 + b] * right for b in range(3)]
        below = jnp.where(at == 0, 0.0, pltpu.roll(s[0], 1, 0))
        above = jnp.where(at == LAT - 1, 0.0, pltpu.roll(s[2], LAT - 1, 0))
        v = s[1] + below + above
        inner = 0.7978845608028654 * (v + 0.044715 * (v * v * v))
        return 0.5 * v * (1.0 + jnp.tanh(inner))

    for lon in range(0, lons, 2):
        both = jnp.concatenate([one_lon(lon), one_lon(lon + 1)], axis=0)
        o_ref[pl.ds(lon * LAT, 2 * LAT), cols] = both.astype(o_ref.dtype)


def first_kernel(has_tail, n_tok, n_w, skip, place_ref, gain_ref, *refs):
    toks, refs = refs[:n_tok], refs[n_tok:]
    ws, refs = refs[:n_w], refs[n_w:]
    fresh = n_tok > 1
    tail_ref = tail_out = normed_out = None
    if has_tail:
        tail_ref, refs = refs[0], refs[1:]
    k_ref, act_ref, refs = refs[0], refs[1], refs[2:]
    if not has_tail:
        tail_out, refs = refs[0], refs[1:]
    if fresh:
        normed_out, refs = refs[0], refs[1:]
    tok, wbuf, hid_a, hid_b, tsem, wsem, nsem = refs
    scen, row, col = place_ref[0], place_ref[1], place_ref[2]
    n, count = pl.program_id(0), pl.num_programs(0)
    rows, d = tok.shape[0], gain_ref.shape[1]
    lead = hid_a.shape[0] - rows
    lons = act_ref.shape[0] // LAT

    def w_copies(step, sub):
        cols = pl.ds(pl.multiple_of((step + skip) * TILE + sub * SUB, SUB), SUB)
        for ref, base, stride, flip in ws_places(ws):
            off = base + stride * (scen if not flip else 1 - scen)
            off = pl.multiple_of(jnp.int32(off), 16)
            pltpu.make_async_copy(
                ref.at[:, cols], wbuf.at[sub, pl.ds(off, ref.shape[0]), :], wsem.at[sub]
            ).start()

    @pl.when(n == 0)
    def _():
        def tok_copy(ref, f):
            at = pl.multiple_of((row ^ f) * d, d)
            pltpu.make_async_copy(ref, tok.at[:, pl.ds(at, d)], tsem).start()

        if fresh:
            tok_copy(toks[0], col)
            for hop in (1, 2, 3):

                @pl.when(col + hop <= 3)
                def _():
                    tok_copy(toks[hop], col + hop)

                @pl.when(col - hop >= 0)
                def _():
                    tok_copy(toks[3 + hop], col - hop)

        else:
            pltpu.make_async_copy(toks[0], tok, tsem).start()
        for sub in range(TILE // SUB):
            w_copies(0, sub)
        pltpu.make_async_copy(tok, tok, tsem).wait()

        def norm(i, _):
            part = pl.ds(pl.multiple_of(i * BLOCK, 16), BLOCK)
            total = square = 0.0
            for j in range(4):
                v = tok[part, pl.ds(j * d, d)].astype(jnp.float32)
                total += jnp.sum(v, axis=1, keepdims=True)
                square += jnp.sum(v * v, axis=1, keepdims=True)
            mean = total / (4 * d)
            scale = lax.rsqrt(square / (4 * d) - mean * mean + eps)
            for j in range(4):
                cols = pl.ds(j * d, d)
                v = (tok[part, cols].astype(jnp.float32) - mean) * scale * gain_ref[pl.ds(row ^ j, 1), :]
                tok[part, cols] = v.astype(jnp.bfloat16)
            return 0

        if fresh:
            lax.fori_loop(0, rows // BLOCK, norm, 0)
            pltpu.make_async_copy(tok, normed_out, nsem).start()

    if fresh:

        @pl.when(n == count - 1)
        def _():
            pltpu.make_async_copy(tok, normed_out, nsem).wait()

    hids = (hid_a, hid_b)
    subs = TILE // SUB
    for sub in range(subs):
        pltpu.make_async_copy(wbuf.at[sub], wbuf.at[sub], wsem.at[sub]).wait()
        hid = hids[sub % 2]
        product = jnp.dot(tok[...], wbuf[sub], preferred_element_type=jnp.float32)
        hidden = product.astype(jnp.bfloat16)
        if has_tail:
            hid[pl.ds(0, lead), :] = tail_ref[:, pl.ds(sub * SUB, SUB)].astype(jnp.float32)
        else:
            tail_out[:, pl.ds(sub * SUB, SUB)] = hidden[rows - 2 * LAT :]
        hid[pl.ds(lead, rows), :] = hidden.astype(jnp.float32)
        if sub > 0:
            conv_gelu(hids[1 - sub % 2], k_ref, act_ref, (sub - 1) * SUB, lons)

        @pl.when(n + 1 < count)
        def _():
            w_copies(n + 1, sub)

    conv_gelu(hids[(subs - 1) % 2], k_ref, act_ref, (subs - 1) * SUB, lons)


def ws_places(ws):
    d = ws[0].shape[0]
    out = [(ws[0], 0, 0, False), (ws[1], d, 0, False)]
    for which in range(2):
        x0, y0, x1, y1, xd = ws[2 + which * 5 : 7 + which * 5]
        base, h = (2 + which) * d, x0.shape[0]
        out += [(x0, base, 2 * h, False), (y0, base, 2 * h, True)]
        out += [(x1, base + h, 2 * h, False), (y1, base + h, 2 * h, True)]
        out += [(xd, base + 4 * h, 0, False)]
    return out


def first(place, gain, toks, ws, conv_kernel, tail, half, lons):
    rows, d = toks[0].shape[0], gain.shape[1]
    units = conv_kernel.shape[1] // 2
    skip = half * (units // TILE)
    has_tail, fresh = tail is not None, len(toks) > 1
    hid_rows = rows + (2 * LAT if has_tail else 0)
    any_spec = pl.BlockSpec(memory_space=pl.ANY)
    wide = lambda r: pl.BlockSpec((r, TILE), lambda n: (0, n))
    shape = lambda r, c: jax.ShapeDtypeStruct((r, c), jnp.bfloat16)
    out_specs, out_shape = [wide(lons * LAT)], [shape(lons * LAT, units)]
    if not has_tail:
        out_specs.append(wide(2 * LAT))
        out_shape.append(shape(2 * LAT, units))
    if fresh:
        out_specs.append(any_spec)
        out_shape.append(shape(rows, 4 * d))
    return pl.pallas_call(
        functools.partial(first_kernel, has_tail, len(toks), len(ws), skip),
        grid=(units // TILE,),
        in_specs=[pl.BlockSpec(memory_space=pltpu.SMEM), pl.BlockSpec(gain.shape, lambda n: (0, 0))]
        + [any_spec] * (len(toks) + len(ws))
        + ([wide(2 * LAT)] if has_tail else [])
        + [pl.BlockSpec((9, TILE), lambda n: (0, n + skip))],
        out_specs=out_specs,
        out_shape=out_shape,
        scratch_shapes=[
            pltpu.VMEM((rows, 4 * d), jnp.bfloat16),
            pltpu.VMEM((TILE // SUB, 4 * d, SUB), jnp.bfloat16),
            pltpu.VMEM((hid_rows, SUB), jnp.float32),
            pltpu.VMEM((hid_rows, SUB), jnp.float32),
            pltpu.SemaphoreType.DMA,
            pltpu.SemaphoreType.DMA((TILE // SUB,)),
            pltpu.SemaphoreType.DMA,
        ],
        compiler_params=pltpu.CompilerParams(vmem_limit_bytes=VMEM_LIMIT),
        cost_estimate=pl.CostEstimate(
            flops=2 * rows * 4 * d * units, bytes_accessed=8 * d * units, transcendentals=0
        ),
        name="first",
    )(place, gain, *toks, *ws, *([tail] if has_tail else []), conv_kernel)


def second_kernel(quarters, place_ref, act_l, act_r, own, sib, *refs):
    pieces, refs = refs[: 4 * len(quarters)], refs[4 * len(quarters) :]
    out_ref, wbuf, buf_l, buf_r, wsem, asem = refs
    scen, row = place_ref[0], place_ref[1]
    n, count = pl.program_id(0), pl.num_programs(0)
    width = out_ref.shape[1] // 2
    half = width // 2
    own_at = pl.multiple_of(scen * half, half)
    other_at = pl.multiple_of((1 - scen) * half, half)

    def copies(step, slot):
        for side in range(2):
            copy_tile(2 * step + side, slot, side * width)

    def copy_tile(tile, slot, at):
        source = row ^ (tile // len(quarters))
        for i, quarter in enumerate(quarters):
            mine = lax.rem(tile, len(quarters)) == i

            for j, ref in ((0, own), (1, sib)):

                @pl.when(mine & (source == j))
                def _():
                    pltpu.make_async_copy(
                        ref.at[:, pl.ds(quarter * width, width)],
                        wbuf.at[slot, :, pl.ds(at, width)],
                        wsem.at[slot],
                    ).start()

            for j in (2, 3):

                @pl.when(mine & (source == j))
                def _():
                    for k, off in ((0, own_at), (1, other_at)):
                        pltpu.make_async_copy(
                            pieces[4 * i + 2 * (j - 2) + k],
                            wbuf.at[slot, :, pl.ds(pl.multiple_of(at + off, half), half)],
                            wsem.at[slot],
                        ).start()

    @pl.when(n == 0)
    def _():
        copies(0, 0)
        loads = [
            pltpu.make_async_copy(ref, buf, asem.at[i])
            for i, (ref, buf) in enumerate(((act_l, buf_l), (act_r, buf_r)))
        ]
        for load in loads:
            load.start()
        copies(1, 1)
        for load in loads:
            load.wait()

    slot = lax.rem(n, 3)

    @pl.when(n + 2 < count)
    def _():
        copies(n + 2, lax.rem(n + 2, 3))

    pltpu.make_async_copy(wbuf.at[slot], wbuf.at[slot], wsem.at[slot]).wait()
    k = act_l.shape[1]
    total = jnp.dot(buf_l[...], wbuf[slot, pl.ds(0, k), :], preferred_element_type=jnp.float32)
    total += jnp.dot(buf_r[...], wbuf[slot, pl.ds(k, k), :], preferred_element_type=jnp.float32)
    out_ref[...] = total.astype(out_ref.dtype)


def second(place, acts, shards, pieces, quarters):
    rows, k = acts[0].shape
    width = shards[0].shape[1] // 4
    count = 4 * len(quarters)
    any_spec = pl.BlockSpec(memory_space=pl.ANY)
    used = [p for quarter in quarters for p in pieces[quarter]]
    return pl.pallas_call(
        functools.partial(second_kernel, quarters),
        grid=(count // 2,),
        in_specs=[pl.BlockSpec(memory_space=pltpu.SMEM)] + [any_spec] * (4 + len(used)),
        out_specs=pl.BlockSpec((rows, 2 * width), lambda n: (0, n)),
        out_shape=jax.ShapeDtypeStruct((rows, count * width), jnp.bfloat16),
        scratch_shapes=[
            pltpu.VMEM((3, 2 * k, 2 * width), jnp.bfloat16),
            pltpu.VMEM((rows, k), jnp.bfloat16),
            pltpu.VMEM((rows, k), jnp.bfloat16),
            pltpu.SemaphoreType.DMA((3,)),
            pltpu.SemaphoreType.DMA((2,)),
        ],
        compiler_params=pltpu.CompilerParams(vmem_limit_bytes=VMEM_LIMIT),
        cost_estimate=pl.CostEstimate(
            flops=4 * rows * k * count * width, bytes_accessed=4 * k * count * width, transcendentals=0
        ),
        name="second",
    )(place, *acts, *shards, *used)


def scatter(v):
    return lax.psum_scatter(v, "col", scatter_dimension=1, tiled=True)


def per_device(tokens, norm_gain, w_in, conv_kernel, w_out):
    rows, d = tokens.shape
    scen, row, col = (lax.axis_index(a) for a in ("scen", "row", "col"))
    place = jnp.stack([scen, row, col]).astype(jnp.int32)
    lons = rows // LAT
    la = lons // 2
    cut = (la + 2) * LAT

    h = (d * 13 // 64) // 16 * 16
    xs_in = [lax.dynamic_slice(w_in, (scen * 2 * h + i * h, 0), (h, w_in.shape[1])) for i in range(2)]
    xs_in.append(w_in[4 * h :])
    q = d // 4
    os_in = [lax.dynamic_slice(w_out, (0, i * q + scen * (q // 2)), (w_out.shape[0], q // 2)) for i in range(4)]
    gain = norm_gain.reshape(4, d)
    wide = extended(tokens, (("row", 0),), LAT)
    na, nb = wide[:cut], wide[cut:]
    (na, nb), (x0i,) = gate((na, nb), (xs_in[0],))
    x0 = swap_x(x0i)
    d1, u1 = down(na, 1), up(na, 1)
    sib = swap_core(w_in)
    (x0, sib, d1, u1), (x1i,) = gate((x0, sib, d1, u1), (xs_in[1],))
    x1, y0 = swap_x(x1i), swap_scen(x0)
    d2, u2 = down(d1, 2), up(u1, 2)
    o_sib, cx0 = cores(w_out, x0)
    (x1, y0, o_sib, cx0, d2, u2), (x2i,) = gate((x1, y0, o_sib, cx0, d2, u2), (xs_in[2],))
    xd, y1 = swap_x(x2i), swap_scen(x1)
    d3, u3 = down(d2, 3), up(u2, 3)
    cy0, cx1 = cores(y0, x1)
    (xd, y1, cy0, cx1, d3, u3), (o0i, nb) = gate((xd, y1, cy0, cx1, d3, u3), (os_in[0], nb))
    ox0 = swap_x(o0i)
    e1, f1 = down(nb, 1), up(nb, 1)
    cxd, cy1 = cores(xd, y1)
    toks_a = [na, d1, d2, d3, u1, u2, u3]
    ws = [w_in, sib, x0, y0, x1, y1, xd, cx0, cy0, cx1, cy1, cxd]
    act_a0, tail0, norm_a = first(place, gain, toks_a, ws, conv_kernel, None, 0, la)
    (norm_a, ox0, e1, f1), (o1i,) = gate((norm_a, ox0, e1, f1), (os_in[1],))
    ox1, oy0 = swap_x(o1i), swap_scen(ox0)
    e2, f2 = down(e1, 2), up(f1, 2)
    cox0 = swap_core(ox0)
    act_a1, tail1 = first(place, gain, [norm_a], ws, conv_kernel, None, 1, la)
    (act_a1, ox1, oy0, cox0, e2, f2), (o2i,) = gate((act_a1, ox1, oy0, cox0, e2, f2), (os_in[2],))
    coy0 = swap_core(oy0)
    ox2, oy1 = swap_x(o2i), swap_scen(ox1)
    e3, f3 = down(e2, 3), up(f2, 3)
    shards = (w_out, o_sib)
    pieces = [(ox0, oy0, cox0, coy0), None, None, None]
    p0 = second(place, (act_a0, act_a1), shards, pieces, (0,))
    r0 = scatter(p0)
    (p0, ox2, oy1, act_a1, e3, f3), (o3i, ox1) = gate((p0, ox2, oy1, act_a1, e3, f3), (os_in[3], ox1))
    ox3, oy2 = swap_x(o3i), swap_scen(ox2)
    coy1, cox1 = cores(oy1, ox1)
    pieces[1] = (ox1, oy1, cox1, coy1)
    p1 = second(place, (act_a0, act_a1), shards, pieces, (1,))
    r1 = scatter(p1)
    (p1, ox3, oy2, r0), (ox2, nb) = gate((p1, ox3, oy2, r0), (ox2, nb))
    oy3 = swap_scen(ox3)
    coy2, cox2 = cores(oy2, ox2)
    toks_b = [nb, e1, e2, e3, f1, f2, f3]
    act_b0, norm_b = first(place, gain, toks_b, ws, conv_kernel, tail0, 0, lons - la)
    (norm_b, oy3, coy2, cox2, act_a1, r1), (ox3,) = gate((norm_b, oy3, coy2, cox2, act_a1, r1), (ox3,))
    coy3, cox3 = cores(oy3, ox3)
    (norm_b, coy3, cox3, act_a1), _ = gate((norm_b, coy3, cox3, act_a1), ())
    pieces[2] = (ox2, oy2, cox2, coy2)
    pieces[3] = (ox3, oy3, cox3, coy3)
    p2 = second(place, (act_a0, act_a1), shards, pieces, (2, 3))
    r2 = scatter(p2)
    (p2, norm_b), _ = gate((p2, norm_b), ())
    (act_b1,) = first(place, gain, [norm_b], ws, conv_kernel, tail1, 1, lons - la)
    s0 = second(place, (act_b0, act_b1), shards, pieces, (0, 1))
    (s0, act_b1, r2), _ = gate((s0, act_b1, r2), ())
    s1 = second(place, (act_b0, act_b1), shards, pieces, (2, 3))
    s0, s1 = scatter(s0), scatter(s1)
    mixed = jnp.concatenate(
        [jnp.concatenate([r0, r1, r2], axis=1), jnp.concatenate([s0, s1], axis=1)], axis=0
    )
    return (tokens.astype(jnp.float32) + mixed.astype(jnp.float32)).astype(jnp.bfloat16)


def solution(mesh):
    placed = (P(("scen", "row"), "col"), P(), P("row", "col"), P(None, "col"), P("col", "row"))
    sizes = tuple(mesh.shape[a] for a in ("scen", "row", "col"))
    return jax.shard_map(
        per_device if sizes == (2, 4, 4) else any_mesh,
        mesh=mesh,
        in_specs=placed,
        out_specs=P(("scen", "row"), "col"),
        check_vma=False,
    )
```

```python
import functools

import jax
import jax.numpy as jnp
from jax import lax
from jax.experimental import pallas as pl
from jax.experimental.pallas import tpu as pltpu
from jax.sharding import PartitionSpec as P

LAT = 40
eps = 1e-05
TILE = 1024
SUB = 512
LANES = 128
BLOCK = 80
VMEM_LIMIT = 58 * 1024 * 1024


def extended(cells, sides, width):
    for axis, dim in sides:
        count = lax.axis_size(axis)
        head = lax.slice_in_dim(cells, 0, width, axis=dim)
        tail = lax.slice_in_dim(cells, cells.shape[dim] - width, cells.shape[dim], axis=dim)
        cells = jnp.concatenate(
            [
                lax.ppermute(tail, axis, [(i, (i + 1) % count) for i in range(count)]),
                cells,
                lax.ppermute(head, axis, [((i + 1) % count, i) for i in range(count)]),
            ],
            axis=dim,
        )
    return cells


def any_mesh(tokens, norm_gain, w_in, conv_kernel, w_out):
    rows, local_cols = tokens.shape
    values = tokens.astype(jnp.float32)
    whole = lax.all_gather(tokens, "col", axis=1, tiled=True).astype(jnp.float32)
    mean = jnp.mean(whole, axis=1, keepdims=True)
    var = jnp.mean(whole * whole, axis=1, keepdims=True) - mean * mean
    normed = ((whole - mean) * lax.rsqrt(var + eps) * norm_gain).astype(jnp.bfloat16)
    units = w_in.shape[1]
    pre_hidden = jnp.dot(
        normed, lax.all_gather(w_in, "row", axis=0, tiled=True), preferred_element_type=jnp.float32
    )
    hidden = pre_hidden.astype(jnp.bfloat16)
    lon_local = rows // LAT
    grid = hidden.reshape(lon_local, LAT, units)
    padded = extended(grid, (("row", 0),), 1)
    padded = jnp.pad(padded.astype(jnp.float32), ((0, 0), (1, 1), (0, 0)))
    conv = jnp.zeros((lon_local, LAT, units), jnp.float32)
    for shift_lon in range(3):
        for shift_lat in range(3):
            conv = (
                conv
                + conv_kernel[shift_lon * 3 + shift_lat]
                * padded[shift_lon : shift_lon + lon_local, shift_lat : shift_lat + LAT]
            )
    act = jax.nn.gelu(conv, approximate=True).astype(jnp.bfloat16).reshape(rows, units)
    partial_value = jnp.dot(
        act, lax.all_gather(w_out, "row", axis=1, tiled=True), preferred_element_type=jnp.float32
    )
    mixed = lax.psum_scatter(partial_value, "col", scatter_dimension=1, tiled=True)
    return (values + mixed).astype(jnp.bfloat16)


def after(value, *others):
    return lax.optimization_barrier((value, *others))[0]


def swap_x(v):
    return lax.ppermute(v, "row", [(i, i ^ 2) for i in range(4)])


def swap_core(v):
    return lax.ppermute(v, "row", [(i, i ^ 1) for i in range(4)])


def cores(*values):
    out = []
    for v in values:
        out.append(swap_core(after(v, *out[-1:])))
    return out


def swap_scen(v):
    return lax.ppermute(v, "scen", [(0, 1), (1, 0)])


def down(v, hop):
    return lax.ppermute(v, "col", [(i, i - 1) for i in range(1, 5 - hop)])


def up(v, hop):
    return lax.ppermute(v, "col", [(i, i + 1) for i in range(hop - 1, 3)])


def gate(done, begin):
    done, begin = lax.optimization_barrier((tuple(done), tuple(begin)))
    return list(done), list(begin)


def conv_gelu(hid_ref, k_ref, o_ref, col, lons):
    for c in range(0, hid_ref.shape[1], LANES):
        conv_gelu_lanes(hid_ref, k_ref, o_ref, c, col + c, lons)


def conv_gelu_lanes(hid_ref, k_ref, o_ref, lane, col, lons):
    width = LANES
    cols, here_cols = pl.ds(col, width), pl.ds(lane, width)
    taps = [k_ref[pl.ds(i, 1), cols] for i in range(9)]
    at = lax.broadcasted_iota(jnp.int32, (LAT, width), 0)

    def one_lon(lon):
        left, here, right = (hid_ref[pl.ds((lon + a) * LAT, LAT), here_cols] for a in range(3))
        s = [taps[b] * left + taps[3 + b] * here + taps[6 + b] * right for b in range(3)]
        below = jnp.where(at == 0, 0.0, pltpu.roll(s[0], 1, 0))
        above = jnp.where(at == LAT - 1, 0.0, pltpu.roll(s[2], LAT - 1, 0))
        v = s[1] + below + above
        inner = 0.7978845608028654 * (v + 0.044715 * (v * v * v))
        return 0.5 * v * (1.0 + jnp.tanh(inner))

    for lon in range(0, lons, 2):
        both = jnp.concatenate([one_lon(lon), one_lon(lon + 1)], axis=0)
        o_ref[pl.ds(lon * LAT, 2 * LAT), cols] = both.astype(o_ref.dtype)


def first_kernel(has_tail, n_tok, n_w, skip, place_ref, gain_ref, *refs):
    toks, refs = refs[:n_tok], refs[n_tok:]
    ws, refs = refs[:n_w], refs[n_w:]
    fresh = n_tok > 1
    tail_ref = tail_out = normed_out = None
    if has_tail:
        tail_ref, refs = refs[0], refs[1:]
    k_ref, act_ref, refs = refs[0], refs[1], refs[2:]
    if not has_tail:
        tail_out, refs = refs[0], refs[1:]
    if fresh:
        normed_out, refs = refs[0], refs[1:]
    tok, wbuf, hid_a, hid_b, tsem, wsem, nsem = refs
    scen, row, col = place_ref[0], place_ref[1], place_ref[2]
    n, count = pl.program_id(0), pl.num_programs(0)
    rows, d = tok.shape[0], gain_ref.shape[1]
    lead = hid_a.shape[0] - rows
    lons = act_ref.shape[0] // LAT

    def w_copies(step, sub):
        cols = pl.ds(pl.multiple_of((step + skip) * TILE + sub * SUB, SUB), SUB)
        for ref, base, stride, flip in ws_places(ws):
            off = base + stride * (scen if not flip else 1 - scen)
            off = pl.multiple_of(jnp.int32(off), 16)
            pltpu.make_async_copy(
                ref.at[:, cols], wbuf.at[sub, pl.ds(off, ref.shape[0]), :], wsem.at[sub]
            ).start()

    @pl.when(n == 0)
    def _():
        def tok_copy(ref, f):
            at = pl.multiple_of((row ^ f) * d, d)
            pltpu.make_async_copy(ref, tok.at[:, pl.ds(at, d)], tsem).start()

        if fresh:
            tok_copy(toks[0], col)
            for hop in (1, 2, 3):

                @pl.when(col + hop <= 3)
                def _():
                    tok_copy(toks[hop], col + hop)

                @pl.when(col - hop >= 0)
                def _():
                    tok_copy(toks[3 + hop], col - hop)

        else:
            pltpu.make_async_copy(toks[0], tok, tsem).start()
        for sub in range(TILE // SUB):
            w_copies(0, sub)
        pltpu.make_async_copy(tok, tok, tsem).wait()

        def norm(i, _):
            part = pl.ds(pl.multiple_of(i * BLOCK, 16), BLOCK)
            total = square = 0.0
            for j in range(4):
                v = tok[part, pl.ds(j * d, d)].astype(jnp.float32)
                total += jnp.sum(v, axis=1, keepdims=True)
                square += jnp.sum(v * v, axis=1, keepdims=True)
            mean = total / (4 * d)
            scale = lax.rsqrt(square / (4 * d) - mean * mean + eps)
            for j in range(4):
                cols = pl.ds(j * d, d)
                v = (tok[part, cols].astype(jnp.float32) - mean) * scale * gain_ref[pl.ds(row ^ j, 1), :]
                tok[part, cols] = v.astype(jnp.bfloat16)
            return 0

        if fresh:
            lax.fori_loop(0, rows // BLOCK, norm, 0)
            pltpu.make_async_copy(tok, normed_out, nsem).start()

    if fresh:

        @pl.when(n == count - 1)
        def _():
            pltpu.make_async_copy(tok, normed_out, nsem).wait()

    hids = (hid_a, hid_b)
    subs = TILE // SUB
    for sub in range(subs):
        pltpu.make_async_copy(wbuf.at[sub], wbuf.at[sub], wsem.at[sub]).wait()
        hid = hids[sub % 2]
        product = jnp.dot(tok[...], wbuf[sub], preferred_element_type=jnp.float32)
        hidden = product.astype(jnp.bfloat16)
        if has_tail:
            hid[pl.ds(0, lead), :] = tail_ref[:, pl.ds(sub * SUB, SUB)].astype(jnp.float32)
        else:
            tail_out[:, pl.ds(sub * SUB, SUB)] = hidden[rows - 2 * LAT :]
        hid[pl.ds(lead, rows), :] = hidden.astype(jnp.float32)
        if sub > 0:
            conv_gelu(hids[1 - sub % 2], k_ref, act_ref, (sub - 1) * SUB, lons)

        @pl.when(n + 1 < count)
        def _():
            w_copies(n + 1, sub)

    conv_gelu(hids[(subs - 1) % 2], k_ref, act_ref, (subs - 1) * SUB, lons)


def ws_places(ws):
    d = ws[0].shape[0]
    out = [(ws[0], 0, 0, False), (ws[1], d, 0, False)]
    for which in range(2):
        x0, y0, x1, y1, xd = ws[2 + which * 5 : 7 + which * 5]
        base, h = (2 + which) * d, x0.shape[0]
        out += [(x0, base, 2 * h, False), (y0, base, 2 * h, True)]
        out += [(x1, base + h, 2 * h, False), (y1, base + h, 2 * h, True)]
        out += [(xd, base + 4 * h, 0, False)]
    return out


def first(place, gain, toks, ws, conv_kernel, tail, half, lons):
    rows, d = toks[0].shape[0], gain.shape[1]
    units = conv_kernel.shape[1] // 2
    skip = half * (units // TILE)
    has_tail, fresh = tail is not None, len(toks) > 1
    hid_rows = rows + (2 * LAT if has_tail else 0)
    any_spec = pl.BlockSpec(memory_space=pl.ANY)
    wide = lambda r: pl.BlockSpec((r, TILE), lambda n: (0, n))
    shape = lambda r, c: jax.ShapeDtypeStruct((r, c), jnp.bfloat16)
    out_specs, out_shape = [wide(lons * LAT)], [shape(lons * LAT, units)]
    if not has_tail:
        out_specs.append(wide(2 * LAT))
        out_shape.append(shape(2 * LAT, units))
    if fresh:
        out_specs.append(any_spec)
        out_shape.append(shape(rows, 4 * d))
    return pl.pallas_call(
        functools.partial(first_kernel, has_tail, len(toks), len(ws), skip),
        grid=(units // TILE,),
        in_specs=[pl.BlockSpec(memory_space=pltpu.SMEM), pl.BlockSpec(gain.shape, lambda n: (0, 0))]
        + [any_spec] * (len(toks) + len(ws))
        + ([wide(2 * LAT)] if has_tail else [])
        + [pl.BlockSpec((9, TILE), lambda n: (0, n + skip))],
        out_specs=out_specs,
        out_shape=out_shape,
        scratch_shapes=[
            pltpu.VMEM((rows, 4 * d), jnp.bfloat16),
            pltpu.VMEM((TILE // SUB, 4 * d, SUB), jnp.bfloat16),
            pltpu.VMEM((hid_rows, SUB), jnp.float32),
            pltpu.VMEM((hid_rows, SUB), jnp.float32),
            pltpu.SemaphoreType.DMA,
            pltpu.SemaphoreType.DMA((TILE // SUB,)),
            pltpu.SemaphoreType.DMA,
        ],
        compiler_params=pltpu.CompilerParams(vmem_limit_bytes=VMEM_LIMIT),
        cost_estimate=pl.CostEstimate(
            flops=2 * rows * 4 * d * units, bytes_accessed=8 * d * units, transcendentals=0
        ),
        name="first",
    )(place, gain, *toks, *ws, *([tail] if has_tail else []), conv_kernel)


def second_kernel(quarters, parts, place_ref, act_l, act_r, own, sib, *refs):
    pieces, refs = refs[: sum(parts)], refs[sum(parts) :]
    out_ref, wbuf, buf_l, buf_r, wsem, asem = refs
    scen, row = place_ref[0], place_ref[1]
    n, count = pl.program_id(0), pl.num_programs(0)
    width = out_ref.shape[1] // 2
    half = width // 2
    own_at = pl.multiple_of(scen * half, half)
    other_at = pl.multiple_of((1 - scen) * half, half)

    def copies(step, slot):
        for side in range(2):
            copy_tile(2 * step + side, slot, side * width)

    def copy_tile(tile, slot, at):
        source = row ^ (tile // len(quarters))
        for i, quarter in enumerate(quarters):
            mine = lax.rem(tile, len(quarters)) == i

            for j, ref in ((0, own), (1, sib)):

                @pl.when(mine & (source == j))
                def _():
                    pltpu.make_async_copy(
                        ref.at[:, pl.ds(quarter * width, width)],
                        wbuf.at[slot, :, pl.ds(at, width)],
                        wsem.at[slot],
                    ).start()

            part = pieces[sum(parts[:i]) : sum(parts[: i + 1])]
            for j in (2, 3):
                share = part[len(part) // 2 * (j - 2) : len(part) // 2 * (j - 1)]
                spots = ((own_at, half), (other_at, half)) if len(share) == 2 else ((0, width),)

                @pl.when(mine & (source == j))
                def _():
                    for ref, (off, wide) in zip(share, spots):
                        pltpu.make_async_copy(
                            ref,
                            wbuf.at[slot, :, pl.ds(pl.multiple_of(at + off, wide), wide)],
                            wsem.at[slot],
                        ).start()

    @pl.when(n == 0)
    def _():
        copies(0, 0)
        loads = [
            pltpu.make_async_copy(ref, buf, asem.at[i])
            for i, (ref, buf) in enumerate(((act_l, buf_l), (act_r, buf_r)))
        ]
        for load in loads:
            load.start()
        copies(1, 1)
        for load in loads:
            load.wait()

    slot = lax.rem(n, 3)

    @pl.when(n + 2 < count)
    def _():
        copies(n + 2, lax.rem(n + 2, 3))

    pltpu.make_async_copy(wbuf.at[slot], wbuf.at[slot], wsem.at[slot]).wait()
    k = act_l.shape[1]
    total = jnp.dot(buf_l[...], wbuf[slot, pl.ds(0, k), :], preferred_element_type=jnp.float32)
    total += jnp.dot(buf_r[...], wbuf[slot, pl.ds(k, k), :], preferred_element_type=jnp.float32)
    out_ref[...] = total.astype(out_ref.dtype)


def second(place, acts, shards, pieces, quarters):
    rows, k = acts[0].shape
    width = shards[0].shape[1] // 4
    count = 4 * len(quarters)
    any_spec = pl.BlockSpec(memory_space=pl.ANY)
    used = [p for quarter in quarters for p in pieces[quarter]]
    return pl.pallas_call(
        functools.partial(second_kernel, quarters, tuple(len(pieces[quarter]) for quarter in quarters)),
        grid=(count // 2,),
        in_specs=[pl.BlockSpec(memory_space=pltpu.SMEM)] + [any_spec] * (4 + len(used)),
        out_specs=pl.BlockSpec((rows, 2 * width), lambda n: (0, n)),
        out_shape=jax.ShapeDtypeStruct((rows, count * width), jnp.bfloat16),
        scratch_shapes=[
            pltpu.VMEM((3, 2 * k, 2 * width), jnp.bfloat16),
            pltpu.VMEM((rows, k), jnp.bfloat16),
            pltpu.VMEM((rows, k), jnp.bfloat16),
            pltpu.SemaphoreType.DMA((3,)),
            pltpu.SemaphoreType.DMA((2,)),
        ],
        compiler_params=pltpu.CompilerParams(vmem_limit_bytes=VMEM_LIMIT),
        cost_estimate=pl.CostEstimate(
            flops=4 * rows * k * count * width, bytes_accessed=4 * k * count * width, transcendentals=0
        ),
        name="second",
    )(place, *acts, *shards, *used)


def scatter(v):
    return lax.psum_scatter(v, "col", scatter_dimension=1, tiled=True)


def per_device(tokens, norm_gain, w_in, conv_kernel, w_out):
    rows, d = tokens.shape
    scen, row, col = (lax.axis_index(a) for a in ("scen", "row", "col"))
    place = jnp.stack([scen, row, col]).astype(jnp.int32)
    lons = rows // LAT
    la = lons * 9 // 32 * 2
    cut = (la + 2) * LAT

    h = (d * 13 // 64) // 16 * 16
    xs_in = [lax.dynamic_slice(w_in, (scen * 2 * h + i * h, 0), (h, w_in.shape[1])) for i in range(2)]
    xs_in.append(w_in[4 * h :])
    q = d // 4
    os_in = [lax.dynamic_slice(w_out, (0, i * q + scen * (q // 2)), (w_out.shape[0], q // 2)) for i in range(3)]
    os_in.append(w_out[:, 3 * q :])
    gain = norm_gain.reshape(4, d)
    wide = extended(tokens, (("row", 0),), LAT)
    na, nb = wide[:cut], wide[cut:]
    (na, nb), (x0i,) = gate((na, nb), (xs_in[0],))
    x0 = swap_x(x0i)
    d1, u1 = down(na, 1), up(na, 1)
    sib = swap_core(w_in)
    (x0, sib, d1, u1), (x1i,) = gate((x0, sib, d1, u1), (xs_in[1],))
    x1, y0 = swap_x(x1i), swap_scen(x0)
    d2, u2 = down(d1, 2), up(u1, 2)
    o_sib, cx0 = cores(w_out, x0)
    (x1, y0, o_sib, cx0, d2, u2), (x2i,) = gate((x1, y0, o_sib, cx0, d2, u2), (xs_in[2],))
    xd, y1 = swap_x(x2i), swap_scen(x1)
    d3, u3 = down(d2, 3), up(u2, 3)
    cy0, cx1 = cores(y0, x1)
    (xd, y1, cy0, cx1, d3, u3, *os_in), (o0i, nb) = gate((xd, y1, cy0, cx1, d3, u3, *os_in), (os_in[0], nb))
    ox0 = swap_x(o0i)
    e1, f1 = down(nb, 1), up(nb, 1)
    cxd, cy1 = cores(xd, y1)
    toks_a = [na, d1, d2, d3, u1, u2, u3]
    ws = [w_in, sib, x0, y0, x1, y1, xd, cx0, cy0, cx1, cy1, cxd]
    act_a0, tail0, norm_a = first(place, gain, toks_a, ws, conv_kernel, None, 0, la)
    (norm_a, ox0, e1, f1), (o1i,) = gate((norm_a, ox0, e1, f1), (os_in[1],))
    ox1, oy0 = swap_x(o1i), swap_scen(ox0)
    e2, f2 = down(e1, 2), up(f1, 2)
    cox0 = swap_core(ox0)
    act_a1, tail1 = first(place, gain, [norm_a], ws, conv_kernel, None, 1, la)
    (act_a1, ox1, oy0, cox0, e2, f2), (o2i,) = gate((act_a1, ox1, oy0, cox0, e2, f2), (os_in[2],))
    coy0 = swap_core(oy0)
    ox2, oy1 = swap_x(o2i), swap_scen(ox1)
    e3, f3 = down(e2, 3), up(f2, 3)
    shards = (w_out, o_sib)
    pieces = [(ox0, oy0, cox0, coy0), None, None, None]
    p0 = second(place, (act_a0, act_a1), shards, pieces, (0,))
    r0 = scatter(p0)
    (p0, ox2, oy1, act_a1, e3, f3), (o3i, ox1) = gate((p0, ox2, oy1, act_a1, e3, f3), (os_in[3], ox1))
    ox3, oy2 = swap_x(o3i), swap_scen(ox2)
    coy1, cox1 = cores(oy1, ox1)
    pieces[1] = (ox1, oy1, cox1, coy1)
    p1 = second(place, (act_a0, act_a1), shards, pieces, (1,))
    r1 = scatter(p1)
    (p1,), (ox2, nb) = gate((p1,), (ox2, nb))
    cox2 = swap_core(ox2)
    toks_b = [nb, e1, e2, e3, f1, f2, f3]
    act_b0, norm_b = first(place, gain, toks_b, ws, conv_kernel, tail0, 0, lons - la)
    (norm_b, ox3, oy2, cox2, r0), (act_a1,) = gate((norm_b, ox3, oy2, cox2, r0), (act_a1,))
    coy2, cox3 = cores(oy2, ox3)
    pieces[2] = (ox2, oy2, cox2, coy2)
    p2 = second(place, (act_a0, act_a1), shards, pieces, (2,))
    r2 = scatter(p2)
    (p2, cox3, r1), (act_a1,) = gate((p2, cox3, r1), (act_a1,))
    pieces[3] = (ox3, cox3)
    p3 = second(place, (act_a0, act_a1), shards, pieces, (3,))
    r3 = scatter(p3)
    (p3, norm_b), _ = gate((p3, norm_b), ())
    (act_b1,) = first(place, gain, [norm_b], ws, conv_kernel, tail1, 1, lons - la)
    s = scatter(second(place, (act_b0, act_b1), shards, pieces, (0, 1, 2, 3)))
    mixed = jnp.concatenate([jnp.concatenate([r0, r1, r2, r3], axis=1), s], axis=0)
    return (tokens.astype(jnp.float32) + mixed.astype(jnp.float32)).astype(jnp.bfloat16)


def solution(mesh):
    placed = (P(("scen", "row"), "col"), P(), P("row", "col"), P(None, "col"), P("col", "row"))
    sizes = tuple(mesh.shape[a] for a in ("scen", "row", "col"))
    return jax.shard_map(
        per_device if sizes == (2, 4, 4) else any_mesh,
        mesh=mesh,
        in_specs=placed,
        out_specs=P(("scen", "row"), "col"),
        check_vma=False,
    )
```

```python
import functools

import jax
import jax.numpy as jnp
from jax import lax
from jax.experimental import pallas as pl
from jax.experimental.pallas import tpu as pltpu
from jax.sharding import PartitionSpec as P

LAT = 40
eps = 1e-05
TILE = 1024
SUB = 512
LANES = 128
BLOCK = 80
VMEM_LIMIT = 58 * 1024 * 1024


def extended(cells, sides, width):
    for axis, dim in sides:
        count = lax.axis_size(axis)
        head = lax.slice_in_dim(cells, 0, width, axis=dim)
        tail = lax.slice_in_dim(cells, cells.shape[dim] - width, cells.shape[dim], axis=dim)
        cells = jnp.concatenate(
            [
                lax.ppermute(tail, axis, [(i, (i + 1) % count) for i in range(count)]),
                cells,
                lax.ppermute(head, axis, [((i + 1) % count, i) for i in range(count)]),
            ],
            axis=dim,
        )
    return cells


def any_mesh(tokens, norm_gain, w_in, conv_kernel, w_out):
    rows, local_cols = tokens.shape
    values = tokens.astype(jnp.float32)
    whole = lax.all_gather(tokens, "col", axis=1, tiled=True).astype(jnp.float32)
    mean = jnp.mean(whole, axis=1, keepdims=True)
    var = jnp.mean(whole * whole, axis=1, keepdims=True) - mean * mean
    normed = ((whole - mean) * lax.rsqrt(var + eps) * norm_gain).astype(jnp.bfloat16)
    units = w_in.shape[1]
    pre_hidden = jnp.dot(
        normed, lax.all_gather(w_in, "row", axis=0, tiled=True), preferred_element_type=jnp.float32
    )
    hidden = pre_hidden.astype(jnp.bfloat16)
    lon_local = rows // LAT
    grid = hidden.reshape(lon_local, LAT, units)
    padded = extended(grid, (("row", 0),), 1)
    padded = jnp.pad(padded.astype(jnp.float32), ((0, 0), (1, 1), (0, 0)))
    conv = jnp.zeros((lon_local, LAT, units), jnp.float32)
    for shift_lon in range(3):
        for shift_lat in range(3):
            conv = (
                conv
                + conv_kernel[shift_lon * 3 + shift_lat]
                * padded[shift_lon : shift_lon + lon_local, shift_lat : shift_lat + LAT]
            )
    act = jax.nn.gelu(conv, approximate=True).astype(jnp.bfloat16).reshape(rows, units)
    partial_value = jnp.dot(
        act, lax.all_gather(w_out, "row", axis=1, tiled=True), preferred_element_type=jnp.float32
    )
    mixed = lax.psum_scatter(partial_value, "col", scatter_dimension=1, tiled=True)
    return (values + mixed).astype(jnp.bfloat16)


def after(value, *others):
    return lax.optimization_barrier((value, *others))[0]


def swap_x(v):
    return lax.ppermute(v, "row", [(i, i ^ 2) for i in range(4)])


def swap_core(v):
    return lax.ppermute(v, "row", [(i, i ^ 1) for i in range(4)])


def cores(*values):
    out = []
    for v in values:
        out.append(swap_core(after(v, *out[-1:])))
    return out


def swap_scen(v):
    return lax.ppermute(v, "scen", [(0, 1), (1, 0)])


def down(v, hop):
    return lax.ppermute(v, "col", [(i, i - 1) for i in range(1, 5 - hop)])


def up(v, hop):
    return lax.ppermute(v, "col", [(i, i + 1) for i in range(hop - 1, 3)])


def gate(done, begin):
    done, begin = lax.optimization_barrier((tuple(done), tuple(begin)))
    return list(done), list(begin)


def conv_gelu(hid_ref, k_ref, o_ref, col, lons):
    for c in range(0, hid_ref.shape[1], LANES):
        conv_gelu_lanes(hid_ref, k_ref, o_ref, c, col + c, lons)


def conv_gelu_lanes(hid_ref, k_ref, o_ref, lane, col, lons):
    width = LANES
    cols, here_cols = pl.ds(col, width), pl.ds(lane, width)
    taps = [k_ref[pl.ds(i, 1), cols] for i in range(9)]
    at = lax.broadcasted_iota(jnp.int32, (LAT, width), 0)

    def one_lon(lon):
        left, here, right = (hid_ref[pl.ds((lon + a) * LAT, LAT), here_cols] for a in range(3))
        s = [taps[b] * left + taps[3 + b] * here + taps[6 + b] * right for b in range(3)]
        below = jnp.where(at == 0, 0.0, pltpu.roll(s[0], 1, 0))
        above = jnp.where(at == LAT - 1, 0.0, pltpu.roll(s[2], LAT - 1, 0))
        v = s[1] + below + above
        inner = 0.7978845608028654 * (v + 0.044715 * (v * v * v))
        return 0.5 * v * (1.0 + jnp.tanh(inner))

    for lon in range(0, lons, 2):
        both = jnp.concatenate([one_lon(lon), one_lon(lon + 1)], axis=0)
        o_ref[pl.ds(lon * LAT, 2 * LAT), cols] = both.astype(o_ref.dtype)


def first_kernel(has_tail, n_tok, n_w, skip, place_ref, gain_ref, *refs):
    toks, refs = refs[:n_tok], refs[n_tok:]
    ws, refs = refs[:n_w], refs[n_w:]
    fresh = n_tok > 1
    tail_ref = tail_out = normed_out = None
    if has_tail:
        tail_ref, refs = refs[0], refs[1:]
    k_ref, act_ref, refs = refs[0], refs[1], refs[2:]
    if not has_tail:
        tail_out, refs = refs[0], refs[1:]
    if fresh:
        normed_out, refs = refs[0], refs[1:]
    tok, wbuf, hid_a, hid_b, tsem, wsem, nsem = refs
    scen, row, col = place_ref[0], place_ref[1], place_ref[2]
    n, count = pl.program_id(0), pl.num_programs(0)
    rows, d = tok.shape[0], gain_ref.shape[1]
    lead = hid_a.shape[0] - rows
    lons = act_ref.shape[0] // LAT

    def w_copies(step, sub):
        cols = pl.ds(pl.multiple_of((step + skip) * TILE + sub * SUB, SUB), SUB)
        for ref, base, stride, flip in ws_places(ws):
            off = base + stride * (scen if not flip else 1 - scen)
            off = pl.multiple_of(jnp.int32(off), 16)
            pltpu.make_async_copy(
                ref.at[:, cols], wbuf.at[sub, pl.ds(off, ref.shape[0]), :], wsem.at[sub]
            ).start()

    @pl.when(n == 0)
    def _():
        def tok_copy(ref, f):
            at = pl.multiple_of((row ^ f) * d, d)
            pltpu.make_async_copy(ref, tok.at[:, pl.ds(at, d)], tsem).start()

        if fresh:
            tok_copy(toks[0], col)
            for hop in (1, 2, 3):

                @pl.when(col + hop <= 3)
                def _():
                    tok_copy(toks[hop], col + hop)

                @pl.when(col - hop >= 0)
                def _():
                    tok_copy(toks[3 + hop], col - hop)

        else:
            pltpu.make_async_copy(toks[0], tok, tsem).start()
        for sub in range(TILE // SUB):
            w_copies(0, sub)
        pltpu.make_async_copy(tok, tok, tsem).wait()

        def norm(i, _):
            part = pl.ds(pl.multiple_of(i * BLOCK, 16), BLOCK)
            total = square = 0.0
            for j in range(4):
                v = tok[part, pl.ds(j * d, d)].astype(jnp.float32)
                total += jnp.sum(v, axis=1, keepdims=True)
                square += jnp.sum(v * v, axis=1, keepdims=True)
            mean = total / (4 * d)
            scale = lax.rsqrt(square / (4 * d) - mean * mean + eps)
            for j in range(4):
                cols = pl.ds(j * d, d)
                v = (tok[part, cols].astype(jnp.float32) - mean) * scale * gain_ref[pl.ds(row ^ j, 1), :]
                tok[part, cols] = v.astype(jnp.bfloat16)
            return 0

        if fresh:
            lax.fori_loop(0, rows // BLOCK, norm, 0)
            pltpu.make_async_copy(tok, normed_out, nsem).start()

    if fresh:

        @pl.when(n == count - 1)
        def _():
            pltpu.make_async_copy(tok, normed_out, nsem).wait()

    hids = (hid_a, hid_b)
    subs = TILE // SUB
    for sub in range(subs):
        pltpu.make_async_copy(wbuf.at[sub], wbuf.at[sub], wsem.at[sub]).wait()
        hid = hids[sub % 2]
        product = jnp.dot(tok[...], wbuf[sub], preferred_element_type=jnp.float32)
        hidden = product.astype(jnp.bfloat16)
        if has_tail:
            hid[pl.ds(0, lead), :] = tail_ref[:, pl.ds(sub * SUB, SUB)].astype(jnp.float32)
        else:
            tail_out[:, pl.ds(sub * SUB, SUB)] = hidden[rows - 2 * LAT :]
        hid[pl.ds(lead, rows), :] = hidden.astype(jnp.float32)
        if sub > 0:
            conv_gelu(hids[1 - sub % 2], k_ref, act_ref, (sub - 1) * SUB, lons)

        @pl.when(n + 1 < count)
        def _():
            w_copies(n + 1, sub)

    conv_gelu(hids[(subs - 1) % 2], k_ref, act_ref, (subs - 1) * SUB, lons)


def ws_places(ws):
    d = ws[0].shape[0]
    out = [(ws[0], 0, 0, False), (ws[1], d, 0, False)]
    for which in range(2):
        x0, y0, x1, y1, xd = ws[2 + which * 5 : 7 + which * 5]
        base, h = (2 + which) * d, x0.shape[0]
        out += [(x0, base, 2 * h, False), (y0, base, 2 * h, True)]
        out += [(x1, base + h, 2 * h, False), (y1, base + h, 2 * h, True)]
        out += [(xd, base + 4 * h, 0, False)]
    return out


def first(place, gain, toks, ws, conv_kernel, tail, half, lons):
    rows, d = toks[0].shape[0], gain.shape[1]
    units = conv_kernel.shape[1] // 2
    skip = half * (units // TILE)
    has_tail, fresh = tail is not None, len(toks) > 1
    hid_rows = rows + (2 * LAT if has_tail else 0)
    any_spec = pl.BlockSpec(memory_space=pl.ANY)
    wide = lambda r: pl.BlockSpec((r, TILE), lambda n: (0, n))
    shape = lambda r, c: jax.ShapeDtypeStruct((r, c), jnp.bfloat16)
    out_specs, out_shape = [wide(lons * LAT)], [shape(lons * LAT, units)]
    if not has_tail:
        out_specs.append(wide(2 * LAT))
        out_shape.append(shape(2 * LAT, units))
    if fresh:
        out_specs.append(any_spec)
        out_shape.append(shape(rows, 4 * d))
    return pl.pallas_call(
        functools.partial(first_kernel, has_tail, len(toks), len(ws), skip),
        grid=(units // TILE,),
        in_specs=[pl.BlockSpec(memory_space=pltpu.SMEM), pl.BlockSpec(gain.shape, lambda n: (0, 0))]
        + [any_spec] * (len(toks) + len(ws))
        + ([wide(2 * LAT)] if has_tail else [])
        + [pl.BlockSpec((9, TILE), lambda n: (0, n + skip))],
        out_specs=out_specs,
        out_shape=out_shape,
        scratch_shapes=[
            pltpu.VMEM((rows, 4 * d), jnp.bfloat16),
            pltpu.VMEM((TILE // SUB, 4 * d, SUB), jnp.bfloat16),
            pltpu.VMEM((hid_rows, SUB), jnp.float32),
            pltpu.VMEM((hid_rows, SUB), jnp.float32),
            pltpu.SemaphoreType.DMA,
            pltpu.SemaphoreType.DMA((TILE // SUB,)),
            pltpu.SemaphoreType.DMA,
        ],
        compiler_params=pltpu.CompilerParams(vmem_limit_bytes=VMEM_LIMIT),
        cost_estimate=pl.CostEstimate(
            flops=2 * rows * 4 * d * units, bytes_accessed=8 * d * units, transcendentals=0
        ),
        name="first",
    )(place, gain, *toks, *ws, *([tail] if has_tail else []), conv_kernel)


def second_kernel(quarters, parts, place_ref, act_l, act_r, own, sib, *refs):
    pieces, refs = refs[: sum(parts)], refs[sum(parts) :]
    out_ref, wbuf, buf_l, buf_r, wsem, asem = refs
    scen, row = place_ref[0], place_ref[1]
    n, count = pl.program_id(0), pl.num_programs(0)
    width = out_ref.shape[1] // 2
    half = width // 2
    own_at = pl.multiple_of(scen * half, half)
    other_at = pl.multiple_of((1 - scen) * half, half)

    def copies(step, slot):
        for side in range(2):
            copy_tile(2 * step + side, slot, side * width)

    def copy_tile(tile, slot, at):
        source = row ^ (tile // len(quarters))
        for i, quarter in enumerate(quarters):
            mine = lax.rem(tile, len(quarters)) == i

            for j, ref in ((0, own), (1, sib)):

                @pl.when(mine & (source == j))
                def _():
                    pltpu.make_async_copy(
                        ref.at[:, pl.ds(quarter * width, width)],
                        wbuf.at[slot, :, pl.ds(at, width)],
                        wsem.at[slot],
                    ).start()

            part = pieces[sum(parts[:i]) : sum(parts[: i + 1])]
            for j in (2, 3):
                share = part[len(part) // 2 * (j - 2) : len(part) // 2 * (j - 1)]
                spots = ((own_at, half), (other_at, half)) if len(share) == 2 else ((0, width),)

                @pl.when(mine & (source == j))
                def _():
                    for ref, (off, wide) in zip(share, spots):
                        pltpu.make_async_copy(
                            ref,
                            wbuf.at[slot, :, pl.ds(pl.multiple_of(at + off, wide), wide)],
                            wsem.at[slot],
                        ).start()

    @pl.when(n == 0)
    def _():
        copies(0, 0)
        loads = [
            pltpu.make_async_copy(ref, buf, asem.at[i])
            for i, (ref, buf) in enumerate(((act_l, buf_l), (act_r, buf_r)))
        ]
        for load in loads:
            load.start()
        copies(1, 1)
        for load in loads:
            load.wait()

    slot = lax.rem(n, 3)

    @pl.when(n + 2 < count)
    def _():
        copies(n + 2, lax.rem(n + 2, 3))

    pltpu.make_async_copy(wbuf.at[slot], wbuf.at[slot], wsem.at[slot]).wait()
    k = act_l.shape[1]
    total = jnp.dot(buf_l[...], wbuf[slot, pl.ds(0, k), :], preferred_element_type=jnp.float32)
    total += jnp.dot(buf_r[...], wbuf[slot, pl.ds(k, k), :], preferred_element_type=jnp.float32)
    out_ref[...] = total.astype(out_ref.dtype)


def second(place, acts, shards, pieces, quarters):
    rows, k = acts[0].shape
    width = shards[0].shape[1] // 4
    count = 4 * len(quarters)
    any_spec = pl.BlockSpec(memory_space=pl.ANY)
    used = [p for quarter in quarters for p in pieces[quarter]]
    return pl.pallas_call(
        functools.partial(second_kernel, quarters, tuple(len(pieces[quarter]) for quarter in quarters)),
        grid=(count // 2,),
        in_specs=[pl.BlockSpec(memory_space=pltpu.SMEM)] + [any_spec] * (4 + len(used)),
        out_specs=pl.BlockSpec((rows, 2 * width), lambda n: (0, n)),
        out_shape=jax.ShapeDtypeStruct((rows, count * width), jnp.bfloat16),
        scratch_shapes=[
            pltpu.VMEM((3, 2 * k, 2 * width), jnp.bfloat16),
            pltpu.VMEM((rows, k), jnp.bfloat16),
            pltpu.VMEM((rows, k), jnp.bfloat16),
            pltpu.SemaphoreType.DMA((3,)),
            pltpu.SemaphoreType.DMA((2,)),
        ],
        compiler_params=pltpu.CompilerParams(vmem_limit_bytes=VMEM_LIMIT),
        cost_estimate=pl.CostEstimate(
            flops=4 * rows * k * count * width, bytes_accessed=4 * k * count * width, transcendentals=0
        ),
        name="second",
    )(place, *acts, *shards, *used)


def scatter(v):
    return lax.psum_scatter(v, "col", scatter_dimension=1, tiled=True)


def per_device(tokens, norm_gain, w_in, conv_kernel, w_out):
    rows, d = tokens.shape
    scen, row, col = (lax.axis_index(a) for a in ("scen", "row", "col"))
    place = jnp.stack([scen, row, col]).astype(jnp.int32)
    lons = rows // LAT
    la = lons * 9 // 32 * 2
    cut = (la + 2) * LAT

    h = (d * 13 // 64) // 16 * 16
    xs_in = [lax.dynamic_slice(w_in, (scen * 2 * h + i * h, 0), (h, w_in.shape[1])) for i in range(2)]
    xs_in.append(w_in[4 * h :])
    q = d // 4
    os_in = [lax.dynamic_slice(w_out, (0, i * q + scen * (q // 2)), (w_out.shape[0], q // 2)) for i in range(3)]
    os_in.append(w_out[:, 3 * q :])
    gain = norm_gain.reshape(4, d)
    wide = extended(tokens, (("row", 0),), LAT)
    na, nb = wide[:cut], wide[cut:]
    (na, nb), (x0i,) = gate((na, nb), (xs_in[0],))
    x0 = swap_x(x0i)
    d1, u1 = down(na, 1), up(na, 1)
    sib = swap_core(w_in)
    (x0, sib, d1, u1), (x1i,) = gate((x0, sib, d1, u1), (xs_in[1],))
    x1, y0 = swap_x(x1i), swap_scen(x0)
    d2, u2 = down(d1, 2), up(u1, 2)
    o_sib, cx0 = cores(w_out, x0)
    (x1, y0, o_sib, cx0, d2, u2), (x2i,) = gate((x1, y0, o_sib, cx0, d2, u2), (xs_in[2],))
    xd, y1 = swap_x(x2i), swap_scen(x1)
    d3, u3 = down(d2, 3), up(u2, 3)
    cy0, cx1 = cores(y0, x1)
    (xd, y1, cy0, cx1, d3, u3, *os_in), (o0i, nb) = gate((xd, y1, cy0, cx1, d3, u3, *os_in), (os_in[0], nb))
    ox0 = swap_x(o0i)
    e1, f1 = down(nb, 1), up(nb, 1)
    cxd, cy1 = swap_core(xd), swap_core(y1)
    toks_a = [na, d1, d2, d3, u1, u2, u3]
    ws = [w_in, sib, x0, y0, x1, y1, xd, cx0, cy0, cx1, cy1, cxd]
    act_a0, tail0, norm_a = first(place, gain, toks_a, ws, conv_kernel, None, 0, la)
    (norm_a, ox0, e1, f1), (o1i,) = gate((norm_a, ox0, e1, f1), (os_in[1],))
    ox1, oy0 = swap_x(o1i), swap_scen(ox0)
    e2, f2 = down(e1, 2), up(f1, 2)
    cox0 = swap_core(ox0)
    act_a1, tail1 = first(place, gain, [norm_a], ws, conv_kernel, None, 1, la)
    (act_a1, ox1, oy0, cox0, e2, f2), (o2i,) = gate((act_a1, ox1, oy0, cox0, e2, f2), (os_in[2],))
    coy0 = swap_core(oy0)
    ox2, oy1 = swap_x(o2i), swap_scen(ox1)
    e3, f3 = down(e2, 3), up(f2, 3)
    shards = (w_out, o_sib)
    pieces = [(ox0, oy0, cox0, coy0), None, None, None]
    p0 = second(place, (act_a0, act_a1), shards, pieces, (0,))
    r0 = scatter(p0)
    (p0, ox2, oy1, act_a1, e3, f3), (o3i, ox1) = gate((p0, ox2, oy1, act_a1, e3, f3), (os_in[3], ox1))
    ox3, oy2 = swap_x(o3i), swap_scen(ox2)
    coy1, cox1 = cores(oy1, ox1)
    pieces[1] = (ox1, oy1, cox1, coy1)
    p1 = second(place, (act_a0, act_a1), shards, pieces, (1,))
    r1 = scatter(p1)
    (p1,), (ox2, nb) = gate((p1,), (ox2, nb))
    cox2 = swap_core(ox2)
    toks_b = [nb, e1, e2, e3, f1, f2, f3]
    act_b0, norm_b = first(place, gain, toks_b, ws, conv_kernel, tail0, 0, lons - la)
    (norm_b, ox3, oy2, cox2, r0), (act_a1,) = gate((norm_b, ox3, oy2, cox2, r0), (act_a1,))
    coy2, cox3 = cores(oy2, ox3)
    pieces[2] = (ox2, oy2, cox2, coy2)
    p2 = second(place, (act_a0, act_a1), shards, pieces, (2,))
    r2 = scatter(p2)
    (p2, cox3, r1), (act_a1,) = gate((p2, cox3, r1), (act_a1,))
    pieces[3] = (ox3, cox3)
    p3 = second(place, (act_a0, act_a1), shards, pieces, (3,))
    r3 = scatter(p3)
    (p3, norm_b), _ = gate((p3, norm_b), ())
    (act_b1,) = first(place, gain, [norm_b], ws, conv_kernel, tail1, 1, lons - la)
    s = scatter(second(place, (act_b0, act_b1), shards, pieces, (0, 1, 2, 3)))
    top = tokens[: la * LAT].astype(jnp.float32) + jnp.concatenate([r0, r1, r2, r3], axis=1).astype(jnp.float32)
    low = tokens[la * LAT :].astype(jnp.float32) + s.astype(jnp.float32)
    return jnp.concatenate([top.astype(jnp.bfloat16), low.astype(jnp.bfloat16)], axis=0)


def solution(mesh):
    placed = (P(("scen", "row"), "col"), P(), P("row", "col"), P(None, "col"), P("col", "row"))
    sizes = tuple(mesh.shape[a] for a in ("scen", "row", "col"))
    return jax.shard_map(
        per_device if sizes == (2, 4, 4) else any_mesh,
        mesh=mesh,
        in_specs=placed,
        out_specs=P(("scen", "row"), "col"),
        check_vma=False,
    )
```

```python
import functools

import jax
import jax.numpy as jnp
from jax import lax
from jax.experimental import pallas as pl
from jax.experimental.pallas import tpu as pltpu
from jax.sharding import PartitionSpec as P

LAT = 40
eps = 1e-05
TILE = 1024
SUB = 512
LANES = 256
BLOCK = 80
VMEM_LIMIT = 58 * 1024 * 1024


def extended(cells, sides, width):
    for axis, dim in sides:
        count = lax.axis_size(axis)
        head = lax.slice_in_dim(cells, 0, width, axis=dim)
        tail = lax.slice_in_dim(cells, cells.shape[dim] - width, cells.shape[dim], axis=dim)
        cells = jnp.concatenate(
            [
                lax.ppermute(tail, axis, [(i, (i + 1) % count) for i in range(count)]),
                cells,
                lax.ppermute(head, axis, [((i + 1) % count, i) for i in range(count)]),
            ],
            axis=dim,
        )
    return cells


def any_mesh(tokens, norm_gain, w_in, conv_kernel, w_out):
    rows, local_cols = tokens.shape
    values = tokens.astype(jnp.float32)
    whole = lax.all_gather(tokens, "col", axis=1, tiled=True).astype(jnp.float32)
    mean = jnp.mean(whole, axis=1, keepdims=True)
    var = jnp.mean(whole * whole, axis=1, keepdims=True) - mean * mean
    normed = ((whole - mean) * lax.rsqrt(var + eps) * norm_gain).astype(jnp.bfloat16)
    units = w_in.shape[1]
    pre_hidden = jnp.dot(
        normed, lax.all_gather(w_in, "row", axis=0, tiled=True), preferred_element_type=jnp.float32
    )
    hidden = pre_hidden.astype(jnp.bfloat16)
    lon_local = rows // LAT
    grid = hidden.reshape(lon_local, LAT, units)
    padded = extended(grid, (("row", 0),), 1)
    padded = jnp.pad(padded.astype(jnp.float32), ((0, 0), (1, 1), (0, 0)))
    conv = jnp.zeros((lon_local, LAT, units), jnp.float32)
    for shift_lon in range(3):
        for shift_lat in range(3):
            conv = (
                conv
                + conv_kernel[shift_lon * 3 + shift_lat]
                * padded[shift_lon : shift_lon + lon_local, shift_lat : shift_lat + LAT]
            )
    act = jax.nn.gelu(conv, approximate=True).astype(jnp.bfloat16).reshape(rows, units)
    partial_value = jnp.dot(
        act, lax.all_gather(w_out, "row", axis=1, tiled=True), preferred_element_type=jnp.float32
    )
    mixed = lax.psum_scatter(partial_value, "col", scatter_dimension=1, tiled=True)
    return (values + mixed).astype(jnp.bfloat16)


def after(value, *others):
    return lax.optimization_barrier((value, *others))[0]


def swap_x(v):
    return lax.ppermute(v, "row", [(i, i ^ 2) for i in range(4)])


def swap_core(v):
    return lax.ppermute(v, "row", [(i, i ^ 1) for i in range(4)])


def cores(*values):
    out = []
    for v in values:
        out.append(swap_core(after(v, *out[-1:])))
    return out


def swap_scen(v):
    return lax.ppermute(v, "scen", [(0, 1), (1, 0)])


def down(v, hop):
    return lax.ppermute(v, "col", [(i, i - 1) for i in range(1, 5 - hop)])


def up(v, hop):
    return lax.ppermute(v, "col", [(i, i + 1) for i in range(hop - 1, 3)])


def gate(done, begin):
    done, begin = lax.optimization_barrier((tuple(done), tuple(begin)))
    return list(done), list(begin)


def conv_gelu(hid_ref, k_ref, o_ref, col, lons):
    for c in range(0, hid_ref.shape[1], LANES):
        conv_gelu_lanes(hid_ref, k_ref, o_ref, c, col + c, lons)


def conv_gelu_lanes(hid_ref, k_ref, o_ref, lane, col, lons):
    width = LANES
    cols, here_cols = pl.ds(col, width), pl.ds(lane, width)
    taps = [k_ref[pl.ds(i, 1), cols] for i in range(9)]
    at = lax.broadcasted_iota(jnp.int32, (LAT, width), 0)

    def one_lon(lon):
        left, here, right = (hid_ref[pl.ds((lon + a) * LAT, LAT), here_cols] for a in range(3))
        s = [taps[b] * left + taps[3 + b] * here + taps[6 + b] * right for b in range(3)]
        below = jnp.where(at == 0, 0.0, pltpu.roll(s[0], 1, 0))
        above = jnp.where(at == LAT - 1, 0.0, pltpu.roll(s[2], LAT - 1, 0))
        v = s[1] + below + above
        inner = 0.7978845608028654 * (v + 0.044715 * (v * v * v))
        return 0.5 * v * (1.0 + jnp.tanh(inner))

    for lon in range(0, lons, 2):
        both = jnp.concatenate([one_lon(lon), one_lon(lon + 1)], axis=0)
        o_ref[pl.ds(lon * LAT, 2 * LAT), cols] = both.astype(o_ref.dtype)


def first_kernel(has_tail, n_tok, n_w, skip, place_ref, gain_ref, *refs):
    toks, refs = refs[:n_tok], refs[n_tok:]
    ws, refs = refs[:n_w], refs[n_w:]
    fresh = n_tok > 1
    tail_ref = tail_out = normed_out = None
    if has_tail:
        tail_ref, refs = refs[0], refs[1:]
    k_ref, act_ref, refs = refs[0], refs[1], refs[2:]
    if not has_tail:
        tail_out, refs = refs[0], refs[1:]
    if fresh:
        normed_out, refs = refs[0], refs[1:]
    tok, wbuf, hid_a, hid_b, tsem, wsem, nsem = refs
    scen, row, col = place_ref[0], place_ref[1], place_ref[2]
    n, count = pl.program_id(0), pl.num_programs(0)
    rows, d = tok.shape[0], gain_ref.shape[1]
    lead = hid_a.shape[0] - rows
    lons = act_ref.shape[0] // LAT

    def w_copies(step, sub):
        cols = pl.ds(pl.multiple_of((step + skip) * TILE + sub * SUB, SUB), SUB)
        for ref, base, stride, flip in ws_places(ws):
            off = base + stride * (scen if not flip else 1 - scen)
            off = pl.multiple_of(jnp.int32(off), 16)
            pltpu.make_async_copy(
                ref.at[:, cols], wbuf.at[sub, pl.ds(off, ref.shape[0]), :], wsem.at[sub]
            ).start()

    @pl.when(n == 0)
    def _():
        def tok_copy(ref, f):
            at = pl.multiple_of((row ^ f) * d, d)
            pltpu.make_async_copy(ref, tok.at[:, pl.ds(at, d)], tsem).start()

        if fresh:
            tok_copy(toks[0], col)
            for hop in (1, 2, 3):

                @pl.when(col + hop <= 3)
                def _():
                    tok_copy(toks[hop], col + hop)

                @pl.when(col - hop >= 0)
                def _():
                    tok_copy(toks[3 + hop], col - hop)

        else:
            pltpu.make_async_copy(toks[0], tok, tsem).start()
        for sub in range(TILE // SUB):
            w_copies(0, sub)
        pltpu.make_async_copy(tok, tok, tsem).wait()

        def norm(i, _):
            part = pl.ds(pl.multiple_of(i * BLOCK, 16), BLOCK)
            total = square = 0.0
            for j in range(4):
                v = tok[part, pl.ds(j * d, d)].astype(jnp.float32)
                total += jnp.sum(v, axis=1, keepdims=True)
                square += jnp.sum(v * v, axis=1, keepdims=True)
            mean = total / (4 * d)
            scale = lax.rsqrt(square / (4 * d) - mean * mean + eps)
            for j in range(4):
                cols = pl.ds(j * d, d)
                v = (tok[part, cols].astype(jnp.float32) - mean) * scale * gain_ref[pl.ds(row ^ j, 1), :]
                tok[part, cols] = v.astype(jnp.bfloat16)
            return 0

        if fresh:
            lax.fori_loop(0, rows // BLOCK, norm, 0)
            pltpu.make_async_copy(tok, normed_out, nsem).start()

    if fresh:

        @pl.when(n == count - 1)
        def _():
            pltpu.make_async_copy(tok, normed_out, nsem).wait()

    hids = (hid_a, hid_b)
    subs = TILE // SUB
    for sub in range(subs):
        pltpu.make_async_copy(wbuf.at[sub], wbuf.at[sub], wsem.at[sub]).wait()
        hid = hids[sub % 2]
        product = jnp.dot(tok[...], wbuf[sub], preferred_element_type=jnp.float32)
        hidden = product.astype(jnp.bfloat16)
        if has_tail:
            hid[pl.ds(0, lead), :] = tail_ref[:, pl.ds(sub * SUB, SUB)].astype(jnp.float32)
        else:
            tail_out[:, pl.ds(sub * SUB, SUB)] = hidden[rows - 2 * LAT :]
        hid[pl.ds(lead, rows), :] = hidden.astype(jnp.float32)
        if sub > 0:
            conv_gelu(hids[1 - sub % 2], k_ref, act_ref, (sub - 1) * SUB, lons)

        @pl.when(n + 1 < count)
        def _():
            w_copies(n + 1, sub)

    conv_gelu(hids[(subs - 1) % 2], k_ref, act_ref, (subs - 1) * SUB, lons)


def ws_places(ws):
    d = ws[0].shape[0]
    out = [(ws[0], 0, 0, False), (ws[1], d, 0, False)]
    for which in range(2):
        x0, y0, x1, y1, xd = ws[2 + which * 5 : 7 + which * 5]
        base, h = (2 + which) * d, x0.shape[0]
        out += [(x0, base, 2 * h, False), (y0, base, 2 * h, True)]
        out += [(x1, base + h, 2 * h, False), (y1, base + h, 2 * h, True)]
        out += [(xd, base + 4 * h, 0, False)]
    return out


def first(place, gain, toks, ws, conv_kernel, tail, half, lons):
    rows, d = toks[0].shape[0], gain.shape[1]
    units = conv_kernel.shape[1] // 2
    skip = half * (units // TILE)
    has_tail, fresh = tail is not None, len(toks) > 1
    hid_rows = rows + (2 * LAT if has_tail else 0)
    any_spec = pl.BlockSpec(memory_space=pl.ANY)
    wide = lambda r: pl.BlockSpec((r, TILE), lambda n: (0, n))
    shape = lambda r, c: jax.ShapeDtypeStruct((r, c), jnp.bfloat16)
    out_specs, out_shape = [wide(lons * LAT)], [shape(lons * LAT, units)]
    if not has_tail:
        out_specs.append(wide(2 * LAT))
        out_shape.append(shape(2 * LAT, units))
    if fresh:
        out_specs.append(any_spec)
        out_shape.append(shape(rows, 4 * d))
    return pl.pallas_call(
        functools.partial(first_kernel, has_tail, len(toks), len(ws), skip),
        grid=(units // TILE,),
        in_specs=[pl.BlockSpec(memory_space=pltpu.SMEM), pl.BlockSpec(gain.shape, lambda n: (0, 0))]
        + [any_spec] * (len(toks) + len(ws))
        + ([wide(2 * LAT)] if has_tail else [])
        + [pl.BlockSpec((9, TILE), lambda n: (0, n + skip))],
        out_specs=out_specs,
        out_shape=out_shape,
        scratch_shapes=[
            pltpu.VMEM((rows, 4 * d), jnp.bfloat16),
            pltpu.VMEM((TILE // SUB, 4 * d, SUB), jnp.bfloat16),
            pltpu.VMEM((hid_rows, SUB), jnp.float32),
            pltpu.VMEM((hid_rows, SUB), jnp.float32),
            pltpu.SemaphoreType.DMA,
            pltpu.SemaphoreType.DMA((TILE // SUB,)),
            pltpu.SemaphoreType.DMA,
        ],
        compiler_params=pltpu.CompilerParams(vmem_limit_bytes=VMEM_LIMIT),
        cost_estimate=pl.CostEstimate(
            flops=2 * rows * 4 * d * units, bytes_accessed=8 * d * units, transcendentals=0
        ),
        name="first",
    )(place, gain, *toks, *ws, *([tail] if has_tail else []), conv_kernel)


def second_kernel(quarters, parts, place_ref, act_l, act_r, own, sib, *refs):
    pieces, refs = refs[: sum(parts)], refs[sum(parts) :]
    out_ref, wbuf, buf_l, buf_r, wsem, asem = refs
    scen, row = place_ref[0], place_ref[1]
    n, count = pl.program_id(0), pl.num_programs(0)
    width = out_ref.shape[1] // 2
    half = width // 2
    own_at = pl.multiple_of(scen * half, half)
    other_at = pl.multiple_of((1 - scen) * half, half)

    def copies(step, slot):
        for side in range(2):
            copy_tile(2 * step + side, slot, side * width)

    def copy_tile(tile, slot, at):
        source = row ^ (tile // len(quarters))
        for i, quarter in enumerate(quarters):
            mine = lax.rem(tile, len(quarters)) == i

            for j, ref in ((0, own), (1, sib)):

                @pl.when(mine & (source == j))
                def _():
                    pltpu.make_async_copy(
                        ref.at[:, pl.ds(quarter * width, width)],
                        wbuf.at[slot, :, pl.ds(at, width)],
                        wsem.at[slot],
                    ).start()

            part = pieces[sum(parts[:i]) : sum(parts[: i + 1])]
            for j in (2, 3):
                share = part[len(part) // 2 * (j - 2) : len(part) // 2 * (j - 1)]
                spots = ((own_at, half), (other_at, half)) if len(share) == 2 else ((0, width),)

                @pl.when(mine & (source == j))
                def _():
                    for ref, (off, wide) in zip(share, spots):
                        pltpu.make_async_copy(
                            ref,
                            wbuf.at[slot, :, pl.ds(pl.multiple_of(at + off, wide), wide)],
                            wsem.at[slot],
                        ).start()

    @pl.when(n == 0)
    def _():
        copies(0, 0)
        loads = [
            pltpu.make_async_copy(ref, buf, asem.at[i])
            for i, (ref, buf) in enumerate(((act_l, buf_l), (act_r, buf_r)))
        ]
        for load in loads:
            load.start()
        copies(1, 1)
        for load in loads:
            load.wait()

    slot = lax.rem(n, 3)

    @pl.when(n + 2 < count)
    def _():
        copies(n + 2, lax.rem(n + 2, 3))

    pltpu.make_async_copy(wbuf.at[slot], wbuf.at[slot], wsem.at[slot]).wait()
    k = act_l.shape[1]
    total = jnp.dot(buf_l[...], wbuf[slot, pl.ds(0, k), :], preferred_element_type=jnp.float32)
    total += jnp.dot(buf_r[...], wbuf[slot, pl.ds(k, k), :], preferred_element_type=jnp.float32)
    out_ref[...] = total.astype(out_ref.dtype)


def second(place, acts, shards, pieces, quarters):
    rows, k = acts[0].shape
    width = shards[0].shape[1] // 4
    count = 4 * len(quarters)
    any_spec = pl.BlockSpec(memory_space=pl.ANY)
    used = [p for quarter in quarters for p in pieces[quarter]]
    return pl.pallas_call(
        functools.partial(second_kernel, quarters, tuple(len(pieces[quarter]) for quarter in quarters)),
        grid=(count // 2,),
        in_specs=[pl.BlockSpec(memory_space=pltpu.SMEM)] + [any_spec] * (4 + len(used)),
        out_specs=pl.BlockSpec((rows, 2 * width), lambda n: (0, n)),
        out_shape=jax.ShapeDtypeStruct((rows, count * width), jnp.bfloat16),
        scratch_shapes=[
            pltpu.VMEM((3, 2 * k, 2 * width), jnp.bfloat16),
            pltpu.VMEM((rows, k), jnp.bfloat16),
            pltpu.VMEM((rows, k), jnp.bfloat16),
            pltpu.SemaphoreType.DMA((3,)),
            pltpu.SemaphoreType.DMA((2,)),
        ],
        compiler_params=pltpu.CompilerParams(vmem_limit_bytes=VMEM_LIMIT),
        cost_estimate=pl.CostEstimate(
            flops=4 * rows * k * count * width, bytes_accessed=4 * k * count * width, transcendentals=0
        ),
        name="second",
    )(place, *acts, *shards, *used)


def scatter(v):
    return lax.psum_scatter(v, "col", scatter_dimension=1, tiled=True)


def per_device(tokens, norm_gain, w_in, conv_kernel, w_out):
    rows, d = tokens.shape
    scen, row, col = (lax.axis_index(a) for a in ("scen", "row", "col"))
    place = jnp.stack([scen, row, col]).astype(jnp.int32)
    lons = rows // LAT
    la = lons * 9 // 32 * 2
    cut = (la + 2) * LAT

    h = (d * 13 // 64) // 16 * 16
    xs_in = [lax.dynamic_slice(w_in, (scen * 2 * h + i * h, 0), (h, w_in.shape[1])) for i in range(2)]
    xs_in.append(w_in[4 * h :])
    q = d // 4
    os_in = [lax.dynamic_slice(w_out, (0, i * q + scen * (q // 2)), (w_out.shape[0], q // 2)) for i in range(3)]
    os_in.append(w_out[:, 3 * q :])
    gain = norm_gain.reshape(4, d)
    wide = extended(tokens, (("row", 0),), LAT)
    na, nb = wide[:cut], wide[cut:]
    (na, nb), (x0i,) = gate((na, nb), (xs_in[0],))
    x0 = swap_x(x0i)
    d1, u1 = down(na, 1), up(na, 1)
    sib = swap_core(w_in)
    (x0, sib, d1, u1), (x1i,) = gate((x0, sib, d1, u1), (xs_in[1],))
    x1, y0 = swap_x(x1i), swap_scen(x0)
    d2, u2 = down(d1, 2), up(u1, 2)
    o_sib, cx0 = cores(w_out, x0)
    (x1, y0, o_sib, cx0, d2, u2), (x2i,) = gate((x1, y0, o_sib, cx0, d2, u2), (xs_in[2],))
    xd, y1 = swap_x(x2i), swap_scen(x1)
    d3, u3 = down(d2, 3), up(u2, 3)
    cy0, cx1 = cores(y0, x1)
    (xd, y1, cy0, cx1, d3, u3, *os_in), (o0i, nb) = gate((xd, y1, cy0, cx1, d3, u3, *os_in), (os_in[0], nb))
    ox0 = swap_x(o0i)
    e1, f1 = down(nb, 1), up(nb, 1)
    cxd, cy1 = swap_core(xd), swap_core(y1)
    toks_a = [na, d1, d2, d3, u1, u2, u3]
    ws = [w_in, sib, x0, y0, x1, y1, xd, cx0, cy0, cx1, cy1, cxd]
    act_a0, tail0, norm_a = first(place, gain, toks_a, ws, conv_kernel, None, 0, la)
    (norm_a, ox0, e1, f1), (o1i,) = gate((norm_a, ox0, e1, f1), (os_in[1],))
    ox1, oy0 = swap_x(o1i), swap_scen(ox0)
    e2, f2 = down(e1, 2), up(f1, 2)
    cox0 = swap_core(ox0)
    act_a1, tail1 = first(place, gain, [norm_a], ws, conv_kernel, None, 1, la)
    (act_a1, ox1, oy0, cox0, e2, f2), (o2i,) = gate((act_a1, ox1, oy0, cox0, e2, f2), (os_in[2],))
    coy0 = swap_core(oy0)
    ox2, oy1 = swap_x(o2i), swap_scen(ox1)
    e3, f3 = down(e2, 3), up(f2, 3)
    shards = (w_out, o_sib)
    pieces = [(ox0, oy0, cox0, coy0), None, None, None]
    p0 = second(place, (act_a0, act_a1), shards, pieces, (0,))
    r0 = scatter(p0)
    (p0, ox2, oy1, act_a1, e3, f3), (o3i, ox1) = gate((p0, ox2, oy1, act_a1, e3, f3), (os_in[3], ox1))
    ox3, oy2 = swap_x(o3i), swap_scen(ox2)
    coy1, cox1 = cores(oy1, ox1)
    pieces[1] = (ox1, oy1, cox1, coy1)
    p1 = second(place, (act_a0, act_a1), shards, pieces, (1,))
    r1 = scatter(p1)
    (p1,), (ox2, nb) = gate((p1,), (ox2, nb))
    cox2 = swap_core(ox2)
    toks_b = [nb, e1, e2, e3, f1, f2, f3]
    act_b0, norm_b = first(place, gain, toks_b, ws, conv_kernel, tail0, 0, lons - la)
    (norm_b, ox3, oy2, cox2, r0), (act_a1,) = gate((norm_b, ox3, oy2, cox2, r0), (act_a1,))
    coy2, cox3 = cores(oy2, ox3)
    pieces[2] = (ox2, oy2, cox2, coy2)
    p2 = second(place, (act_a0, act_a1), shards, pieces, (2,))
    r2 = scatter(p2)
    (p2, cox3, r1), (act_a1,) = gate((p2, cox3, r1), (act_a1,))
    pieces[3] = (ox3, cox3)
    p3 = second(place, (act_a0, act_a1), shards, pieces, (3,))
    r3 = scatter(p3)
    (p3, norm_b), _ = gate((p3, norm_b), ())
    (act_b1,) = first(place, gain, [norm_b], ws, conv_kernel, tail1, 1, lons - la)
    s = scatter(second(place, (act_b0, act_b1), shards, pieces, (0, 1, 2, 3)))
    top = tokens[: la * LAT].astype(jnp.float32) + jnp.concatenate([r0, r1, r2, r3], axis=1).astype(jnp.float32)
    low = tokens[la * LAT :].astype(jnp.float32) + s.astype(jnp.float32)
    return jnp.concatenate([top.astype(jnp.bfloat16), low.astype(jnp.bfloat16)], axis=0)


def solution(mesh):
    placed = (P(("scen", "row"), "col"), P(), P("row", "col"), P(None, "col"), P("col", "row"))
    sizes = tuple(mesh.shape[a] for a in ("scen", "row", "col"))
    return jax.shard_map(
        per_device if sizes == (2, 4, 4) else any_mesh,
        mesh=mesh,
        in_specs=placed,
        out_specs=P(("scen", "row"), "col"),
        check_vma=False,
    )
```
